256 devices in a mesh: group: 32 (over y, z), tensor: 8 (over x, core).
Axes of the slice: x: 4, y: 4, z: 8, core: 2. Of those that a mesh axis runs over, the one named last changes fastest.
Arguments:
- stretch_query_rows: bfloat16 [49152, 8192], P('group', 'tensor'), may hold values from -7 to 7
- earlier_token_cache: bfloat16 [1024, 192, 2, 1024], P('group', None, None, 'tensor'), may hold values from -6 to 6
- stretch_cache: bfloat16 [1024, 48, 2, 1024], P('group', None, None, 'tensor'), may hold values from -6 to 6
- stretch_position: int32 [1024], P('group'), may hold values from 16 to 192, as said below
- owning_decode_group: int32 [1024], P('group'), may hold values from 0 to 31, as said below
- decode_query_rows: bfloat16 [2048, 8192], P('group', 'tensor'), may hold values from -7 to 7
- decode_input_rows: bfloat16 [2048, 8192], P('group', 'tensor'), may hold values from -6 to 6
- decode_base_projection: bfloat16 [2048, 2, 1024], P('group', None, 'tensor'), may hold values from -6 to 6
- row_adapter_index: int32 [2048], P('group'), may hold values from 0 to 7
- adapter_down_weight: bfloat16 [8192, 256], P('tensor'), may hold values from -0.0625 to 0.0625
- adapter_up_weight: bfloat16 [256, 1024], P(None, 'tensor'), may hold values from -1.5 to 1.5
- group_page_store: bfloat16 [3072, 16, 2, 1024], P('group', None, None, 'tensor'), may hold values from -6 to 6
- row_page_index: int32 [2048, 15], P('group'), may hold values from 0 to 287, as said below
- cached_token_length: int32 [2048], P('group'), may hold values from 1 to 240
Outputs:
- prefill_out: bfloat16 [49152, 8192], P('group', 'tensor')
- decode_out: bfloat16 [2048, 8192], P('group', 'tensor')
The draws below stay inside these ranges and needn't reach their ends.
Inputs may be any that keep to these rules, and one draw needn't show every extreme that they name: `owning_decode_group`: at most 2 prompts of one prefill group name the same decode group, and some decode group is named by exactly 2 prompts of every group. `stretch_position`: multiples of 16. `row_page_index`: an entry e >= 96 names landing page e - 96 of the row's group, and only pages that hold a prompt's tokens are named. Entries at and beyond position (cached_token_length[r] - 1) // 16 + 1 are not read.
All inputs are finite; a program needn't handle non-finite values.
Results may differ from the reference program's by a relative error of at most 0.02.
Values may be sent and summed in bfloat16 or wider, within the bound.
No kernel may reach another device: no remote copies, remote signals or barrier semaphores. Data moves between devices by JAX's collectives and lax.ppermute only.
A program may use at most 128 MiB of HBM per device.

```python
import jax
import jax.numpy as jnp
from jax import lax

MODEL_WIDTH = 8192
QUERY_HEADS = 64
KEY_VALUE_HEADS = 8
HEAD_SIZE = 128
ADAPTER_RANK = 16
ADAPTER_COUNT = 8
PAGE = 16
STRETCH_TOKENS = 48
PROMPTS_GRP = 32
PREFIX_LENGTH = 192
GROUP_ROWS = 64
POOL = 96
KEY_VALUE_WIDTH = 1024
PAGES_CH = 3
MAXP = 15
CAP = 2
LANDS = 192
PROMPTS = 1024
DECODE_ROWS = 2048
POOLS = 3072
N_GROUP = 32


def make_plan(key):
    key = jax.random.fold_in(key, 900)
    groups = PROMPTS // PROMPTS_GRP
    keys_list = jax.random.split(key, 8)
    hot_group = jax.random.randint(keys_list[0], (), 0, groups, dtype=jnp.int32)

    def one_source(source_key):
        order_key, slot_key = jax.random.split(source_key)
        others = jax.random.permutation(slot_key, (groups - 1) * CAP)[:PROMPTS_GRP - CAP].astype(jnp.int32) // CAP + 1
        listed = jnp.concatenate([jnp.zeros((CAP,), jnp.int32), others])
        return listed[jax.random.permutation(order_key, PROMPTS_GRP)]
    relative = jax.vmap(one_source)(jax.random.split(keys_list[1], groups))
    destinations = (relative + hot_group) % groups
    offsets = PAGE * jax.random.randint(keys_list[2], (groups, PROMPTS_GRP), 1, PREFIX_LENGTH // PAGE + 1, dtype=jnp.int32)
    forced_group = jax.random.randint(keys_list[3], (), 0, groups, dtype=jnp.int32)
    forced_prompt = jax.random.randint(keys_list[4], (), 0, PROMPTS_GRP, dtype=jnp.int32)
    offsets = offsets.at[forced_group, forced_prompt].set(PREFIX_LENGTH)
    same_dest = destinations[:, :, None] == destinations[:, None, :]
    order_index = jnp.arange(PROMPTS_GRP, dtype=jnp.int32)
    earlier = order_index[None, :] < order_index[:, None]
    slot_ranks = jnp.sum((same_dest & earlier[None]).astype(jnp.int32), axis=2)
    landing_base = POOL + (jnp.arange(groups, dtype=jnp.int32)[:, None] * CAP + slot_ranks) * PAGES_CH
    flat_dest = destinations.reshape(-1)
    flat_index = jnp.arange(groups * PROMPTS_GRP, dtype=jnp.int32)
    arrival = jnp.sum(((flat_dest[None, :] == flat_dest[:, None]) & (flat_index[None, :] < flat_index[:, None])).astype(jnp.int32), axis=1)

    def row_order(row_key):
        return jax.random.permutation(row_key, GROUP_ROWS).astype(jnp.int32)
    row_orders = jax.vmap(row_order)(jax.random.split(keys_list[5], groups))
    target_row = row_orders[flat_dest, arrival]
    lengths = jax.random.randint(keys_list[6], (groups, GROUP_ROWS), 1, MAXP * PAGE + 1, dtype=jnp.int32)
    tables = jax.random.randint(keys_list[7], (groups, GROUP_ROWS, MAXP), 0, POOL, dtype=jnp.int32)
    prompt_pages = offsets.reshape(-1) // PAGE
    positions = jnp.arange(MAXP, dtype=jnp.int32)
    chosen_tables = tables[flat_dest, target_row]
    inside = (positions[None, :] >= prompt_pages[:, None]) & (positions[None, :] < prompt_pages[:, None] + PAGES_CH)
    landed = landing_base.reshape(-1)[:, None] + positions[None, :] - prompt_pages[:, None]
    tables = tables.at[flat_dest, target_row].set(jnp.where(inside, landed, chosen_tables))
    lengths = lengths.at[flat_dest, target_row].set(offsets.reshape(-1) + STRETCH_TOKENS)
    return (flat_dest, offsets.reshape(-1), tables.reshape(-1, MAXP), lengths.reshape(-1))


def drawn_queries(key, row_count):
    array_shape = (row_count, QUERY_HEADS * HEAD_SIZE)
    return jnp.clip(jax.random.normal(key, array_shape, jnp.float32), -6.0, 6.0).astype(jnp.bfloat16)


def drawn_keys(key, array_shape):
    return jnp.clip(jax.random.normal(key, array_shape, jnp.float32), -6.0, 6.0).astype(jnp.bfloat16)


def draw_owning_decode_group(key, part):
    return make_plan(key)[0]


def draw_stretch_position(key, part):
    return make_plan(key)[1]


def draw_row_page_index(key, part):
    return make_plan(key)[2]


def draw_cached_token_length(key, part):
    return make_plan(key)[3]


def draw_stretch_query_rows(key, part):
    key = jax.random.fold_in(key, 3)
    return drawn_queries(key, PROMPTS * STRETCH_TOKENS)


def draw_decode_query_rows(key, part):
    key = jax.random.fold_in(key, 5)
    return drawn_queries(key, DECODE_ROWS)


def draw_earlier_token_cache(key, part):
    key = jax.random.fold_in(key, 9)
    return drawn_keys(key, (PROMPTS, PREFIX_LENGTH, 2, KEY_VALUE_WIDTH))


def draw_group_page_store(key, part):
    key = jax.random.fold_in(key, 13)
    return drawn_keys(key, (POOLS, PAGE, 2, KEY_VALUE_WIDTH))


def touch_ends(array, stream_key, low, top_value):
    spot = [jax.random.randint(jax.random.fold_in(stream_key, axis), (), 0, length) for axis, length in enumerate(array.shape)]
    longest = array.shape.index(max(array.shape))
    beside = spot[:longest] + [(spot[longest] + 1) % array.shape[longest]] + spot[longest + 1:]
    return array.at[tuple(spot)].set(low).at[tuple(beside)].set(top_value)


def steps_of(stream_key, dims, pieces, least, high):
    level, own = 1.0, jax.random.fold_in(stream_key, 6)
    for position, blocks in pieces:
        heights = jnp.exp(jax.random.uniform(jax.random.fold_in(own, position), (blocks,), jnp.float32, least / len(pieces), high / len(pieces)))
        level = level * jnp.repeat(heights, dims[position] // blocks).reshape([-1 if axis == position else 1 for axis in range(len(dims))])
    return level


def bell_draw(stream_key, dims, deviation, limit, shards=(), kind=jnp.bfloat16):
    drawn = jax.random.normal(stream_key, dims, jnp.float32) * deviation
    if len(shards) > 0:
        drawn = steps_of(stream_key, dims, shards, -0.22, 0.18) * drawn
    return jnp.clip(drawn, min=-limit, max=limit).astype(kind)


def setup_inputs(seed: int = 0) -> dict:
    keys = jax.random.split(jax.random.key(seed), 15)
    stretch_query_rows = draw_stretch_query_rows(jax.random.fold_in(keys[14], 71), 0)
    earlier_token_cache = draw_earlier_token_cache(jax.random.fold_in(keys[14], 71), 0)
    stretch_cache = bell_draw(keys[2], (PROMPTS, STRETCH_TOKENS, 2, KEY_VALUE_WIDTH), 1.0, 6.0, ((0, 32), (3, 8)))
    stretch_position = draw_stretch_position(jax.random.fold_in(keys[14], 71), 0)
    owning_decode_group = draw_owning_decode_group(jax.random.fold_in(keys[14], 71), 0)
    decode_query_rows = draw_decode_query_rows(jax.random.fold_in(keys[14], 71), 0)
    decode_input_rows = bell_draw(keys[6], (DECODE_ROWS, MODEL_WIDTH), 1.0, 6.0, ((0, 32), (1, 8)))
    decode_base_projection = bell_draw(keys[7], (DECODE_ROWS, 2, KEY_VALUE_WIDTH), 1.0, 6.0, ((0, 32), (2, 8)))
    row_adapter_index = touch_ends(jax.random.randint(keys[8], (DECODE_ROWS,), 0, ADAPTER_COUNT), jax.random.fold_in(keys[8], 1), 0, ADAPTER_COUNT - 1).astype(jnp.int32)
    adapter_down_weight = bell_draw(keys[9], (MODEL_WIDTH, ADAPTER_COUNT * 2 * ADAPTER_RANK), MODEL_WIDTH ** -0.5, 0.0625, ((0, 8),))
    adapter_up_weight = bell_draw(keys[10], (ADAPTER_COUNT * 2 * ADAPTER_RANK, KEY_VALUE_WIDTH), ADAPTER_RANK ** -0.5, 1.5, ((1, 8),))
    group_page_store = draw_group_page_store(jax.random.fold_in(keys[14], 71), 0)
    row_page_index = draw_row_page_index(jax.random.fold_in(keys[14], 71), 0)
    cached_token_length = draw_cached_token_length(jax.random.fold_in(keys[14], 71), 0)
    return {"stretch_query_rows": stretch_query_rows, "earlier_token_cache": earlier_token_cache, "stretch_cache": stretch_cache, "stretch_position": stretch_position, "owning_decode_group": owning_decode_group, "decode_query_rows": decode_query_rows, "decode_input_rows": decode_input_rows, "decode_base_projection": decode_base_projection, "row_adapter_index": row_adapter_index, "adapter_down_weight": adapter_down_weight, "adapter_up_weight": adapter_up_weight, "group_page_store": group_page_store, "row_page_index": row_page_index, "cached_token_length": cached_token_length}


ADAPTER_SCALE = 2.0


def prompt_slots(owning_decode_group):
    group_sorted = owning_decode_group.reshape(-1, PROMPTS_GRP)
    same_dest = group_sorted[:, :, None] == group_sorted[:, None, :]
    order_index = jnp.arange(PROMPTS_GRP, dtype=jnp.int32)
    earlier = order_index[None, :] < order_index[:, None]
    return jnp.sum((same_dest & earlier[None]).astype(jnp.int32), axis=2).reshape(-1)


def prefill_prompt(inputs):
    query_block, prefix_block, stretch_block, offset = inputs
    group_sorted = query_block.astype(jnp.float32).reshape(STRETCH_TOKENS, KEY_VALUE_HEADS, QUERY_HEADS // KEY_VALUE_HEADS, HEAD_SIZE)
    earlier_keys = prefix_block[:, 0].astype(jnp.float32).reshape(PREFIX_LENGTH, KEY_VALUE_HEADS, HEAD_SIZE)
    earlier_values = prefix_block[:, 1].astype(jnp.float32).reshape(PREFIX_LENGTH, KEY_VALUE_HEADS, HEAD_SIZE)
    stretch_keys = stretch_block[:, 0].astype(jnp.float32).reshape(STRETCH_TOKENS, KEY_VALUE_HEADS, HEAD_SIZE)
    stretch_values = stretch_block[:, 1].astype(jnp.float32).reshape(STRETCH_TOKENS, KEY_VALUE_HEADS, HEAD_SIZE)
    score_scale = HEAD_SIZE ** -0.5
    prefix_scores = jnp.einsum("qgmd,tgd->gmqt", group_sorted, earlier_keys) * score_scale
    fresh_scores = jnp.einsum("qgmd,jgd->gmqj", group_sorted, stretch_keys) * score_scale
    seen = jnp.arange(PREFIX_LENGTH, dtype=jnp.int32) < offset
    prefix_scores = jnp.where(seen[None, None, None, :], prefix_scores, -jnp.inf)
    stretch_index = jnp.arange(STRETCH_TOKENS, dtype=jnp.int32)
    causal = stretch_index[None, :] <= stretch_index[:, None]
    fresh_scores = jnp.where(causal[None, None], fresh_scores, -jnp.inf)
    row_maximum = jnp.maximum(prefix_scores.max(-1), fresh_scores.max(-1))
    prefix_exp = jnp.exp(prefix_scores - row_maximum[..., None])
    fresh_exp = jnp.exp(fresh_scores - row_maximum[..., None])
    row_total = prefix_exp.sum(-1) + fresh_exp.sum(-1)
    prefix_weights = (prefix_exp / row_total[..., None]).astype(jnp.bfloat16).astype(jnp.float32)
    fresh_weights = (fresh_exp / row_total[..., None]).astype(jnp.bfloat16).astype(jnp.float32)
    attended = jnp.einsum("gmqt,tgd->qgmd", prefix_weights, earlier_values)
    attended = attended + jnp.einsum("gmqj,jgd->qgmd", fresh_weights, stretch_values)
    return attended.reshape(STRETCH_TOKENS, QUERY_HEADS * HEAD_SIZE).astype(jnp.bfloat16)


def attend_decode(query_block, collected_pages, lengths, appended_key_value):
    cache_extent = MAXP * PAGE
    paged_keys = collected_pages[:, :, :, 0].astype(jnp.float32).reshape(GROUP_ROWS, cache_extent, KEY_VALUE_HEADS, HEAD_SIZE)
    paged_values = collected_pages[:, :, :, 1].astype(jnp.float32).reshape(GROUP_ROWS, cache_extent, KEY_VALUE_HEADS, HEAD_SIZE)
    group_sorted = query_block.astype(jnp.float32).reshape(GROUP_ROWS, KEY_VALUE_HEADS, QUERY_HEADS // KEY_VALUE_HEADS, HEAD_SIZE)
    local_key_value = appended_key_value.astype(jnp.float32).reshape(GROUP_ROWS, 2, KEY_VALUE_HEADS, HEAD_SIZE)
    score_scale = HEAD_SIZE ** -0.5
    cache_scores = jnp.einsum("rgmd,rtgd->rgmt", group_sorted, paged_keys) * score_scale
    own_scores = jnp.einsum("rgmd,rgd->rgm", group_sorted, local_key_value[:, 0]) * score_scale
    visible = jnp.arange(cache_extent, dtype=jnp.int32)[None, :] < lengths[:, None]
    cache_scores = jnp.where(visible[:, None, None, :], cache_scores, -jnp.inf)
    row_maximum = jnp.maximum(cache_scores.max(-1), own_scores)
    cache_exp = jnp.exp(cache_scores - row_maximum[..., None])
    own_exp = jnp.exp(own_scores - row_maximum)
    row_total = cache_exp.sum(-1) + own_exp
    cache_weights = (cache_exp / row_total[..., None]).astype(jnp.bfloat16).astype(jnp.float32)
    own_weights = (own_exp / row_total).astype(jnp.bfloat16).astype(jnp.float32)
    attended = jnp.einsum("rgmt,rtgd->rgmd", cache_weights, paged_values)
    attended = attended + own_weights[..., None] * local_key_value[:, 1][:, :, None, :]
    return attended.reshape(GROUP_ROWS, QUERY_HEADS * HEAD_SIZE).astype(jnp.bfloat16)


def reference(stretch_query_rows, earlier_token_cache, stretch_cache, stretch_position, owning_decode_group, decode_query_rows, decode_input_rows, decode_base_projection, row_adapter_index, adapter_down_weight, adapter_up_weight, group_page_store, row_page_index, cached_token_length):
    prefill_out = lax.map(prefill_prompt, (stretch_query_rows.reshape(PROMPTS, STRETCH_TOKENS, QUERY_HEADS * HEAD_SIZE), earlier_token_cache, stretch_cache, stretch_position))
    prefill_out = prefill_out.reshape(PROMPTS * STRETCH_TOKENS, QUERY_HEADS * HEAD_SIZE)

    down_projected_rows = jnp.dot(decode_input_rows, adapter_down_weight, preferred_element_type=jnp.float32).reshape(DECODE_ROWS, ADAPTER_COUNT, 2 * ADAPTER_RANK)
    choose = row_adapter_index[:, None] == jnp.arange(ADAPTER_COUNT, dtype=jnp.int32)[None, :]
    picked = jnp.sum(jnp.where(choose[:, :, None], down_projected_rows, 0.0), axis=1)
    middle = picked.astype(jnp.bfloat16).astype(jnp.float32)
    broadcast_rows = jnp.where(choose[:, :, None], middle[:, None, :], 0.0).reshape(DECODE_ROWS, ADAPTER_COUNT, 2, ADAPTER_RANK)
    up_weight_rows = adapter_up_weight.astype(jnp.float32).reshape(ADAPTER_COUNT, 2, ADAPTER_RANK, KEY_VALUE_WIDTH)
    adapter_delta = jnp.einsum("bsqo,sqon->bqn", broadcast_rows, up_weight_rows)
    incoming_key_value = (decode_base_projection.astype(jnp.float32) + ADAPTER_SCALE * adapter_delta).astype(jnp.bfloat16)

    slot_ranks = prompt_slots(owning_decode_group)
    sources = jnp.arange(PROMPTS, dtype=jnp.int32) // PROMPTS_GRP

    def decode_group(inputs):
        group_id, pool, table, lengths, query_block, appended_key_value = inputs
        target_slot = jnp.where(owning_decode_group == group_id, sources * CAP + slot_ranks, N_GROUP * CAP)
        landing = jnp.zeros((N_GROUP * CAP, STRETCH_TOKENS, 2, KEY_VALUE_WIDTH), stretch_cache.dtype)
        landing = landing.at[target_slot].set(stretch_cache, mode="drop")
        stacked = jnp.concatenate([pool, landing.reshape(LANDS, PAGE, 2, KEY_VALUE_WIDTH)], axis=0)
        collected_pages = jnp.take(stacked, table, axis=0)
        return attend_decode(query_block, collected_pages, lengths, appended_key_value)

    decode_out = lax.map(decode_group, (
        jnp.arange(N_GROUP, dtype=jnp.int32),
        group_page_store.reshape(N_GROUP, POOL, PAGE, 2, KEY_VALUE_WIDTH),
        row_page_index.reshape(N_GROUP, GROUP_ROWS, MAXP),
        cached_token_length.reshape(N_GROUP, GROUP_ROWS),
        decode_query_rows.reshape(N_GROUP, GROUP_ROWS, QUERY_HEADS * HEAD_SIZE),
        incoming_key_value.reshape(N_GROUP, GROUP_ROWS, 2, KEY_VALUE_WIDTH)))
    return prefill_out, decode_out.reshape(DECODE_ROWS, QUERY_HEADS * HEAD_SIZE)
```

```python
import functools

import jax
import jax.numpy as jnp
from jax import lax
from jax.experimental import pallas as pl
from jax.experimental.pallas import tpu as pltpu
from jax.sharding import PartitionSpec as P

HEAD_SIZE = 128
ADAPTER_RANK = 16
ADAPTER_COUNT = 8
PAGE = 16
CAP = 2
ADAPTER_SCALE = 2.0
SCORE_SCALE = HEAD_SIZE ** (-0.5) * 1.4426950408889634
MASKED = -1e30
VMEM_BYTES = 24 * 1024 * 1024
PACK_BYTES = 56 * 1024 * 1024
PROMPT_BLOCK = 8
HEAD_BLOCK = 4
LANDING_TOKENS = 768

CONTRACT_LAST = (((1,), (1,)), ((), ()))


def in_vmem():
    return pl.BlockSpec(memory_space=pltpu.VMEM)


def in_smem():
    return pl.BlockSpec(memory_space=pltpu.SMEM)


def params(limit=VMEM_BYTES):
    return pltpu.CompilerParams(vmem_limit_bytes=limit)


def cost(flops, moved, exps=0):
    return pl.CostEstimate(flops=flops, bytes_accessed=moved, transcendentals=exps)


def pack_kernel(
    owner_hbm, kv_hbm, out_hbm, owner_ref, kv_ref, split_ref, stage_ref, zero_ref, count_ref, slot_ref,
    owner_sem, kv_sem, out_sem,
):
    prompts, rows, _ = kv_ref.shape
    tokens = rows // 2
    groups, cap = out_hbm.shape[:2]
    parts = kv_sem.shape[0]
    span = prompts // parts
    owner_copy = pltpu.make_async_copy(owner_hbm, owner_ref, owner_sem)
    owner_copy.start()
    kv_copies = [
        pltpu.make_async_copy(
            kv_hbm.at[pl.ds(c * span, span)], kv_ref.at[pl.ds(c * span, span)], kv_sem.at[c]
        )
        for c in range(parts)
    ]
    for copy in kv_copies:
        copy.start()
    zero_ref[...] = jnp.zeros_like(zero_ref)
    for d in range(groups):
        count_ref[d] = 0
    owner_copy.wait()
    for p in range(prompts):
        dest = owner_ref[p]
        rank = count_ref[dest]
        count_ref[dest] = rank + 1
        slot_ref[p] = jnp.minimum(rank, cap - 1)
    for c in range(parts):
        kv_copies[c].wait()
        block = slice(c * span, (c + 1) * span)
        split_ref[block] = kv_ref[block].astype(jnp.float32)
        for p in range(c * span, (c + 1) * span):
            for j in range(2):
                part = split_ref[p, pl.ds(j, tokens, stride=2), :]
                stage_ref[p, j * tokens : (j + 1) * tokens] = part.astype(jnp.bfloat16)
        for p in range(c * span, (c + 1) * span):
            pltpu.make_async_copy(
                stage_ref.at[p], out_hbm.at[owner_ref[p], slot_ref[p]], out_sem
            ).start()
    for d in range(groups):
        for slot in range(cap):

            @pl.when(count_ref[d] <= slot)
            def _():
                pltpu.make_async_copy(zero_ref, out_hbm.at[d, slot], out_sem).start()

    pltpu.make_async_copy(out_hbm, out_hbm, out_sem).wait()


def pack(owner, stretch, groups):
    prompts, rows, _ = stretch.shape
    parts = 4
    return pl.pallas_call(
        pack_kernel,
        out_shape=jax.ShapeDtypeStruct((groups, CAP, rows, HEAD_SIZE), jnp.bfloat16),
        in_specs=[pl.BlockSpec(memory_space=pl.ANY)] * 2,
        out_specs=pl.BlockSpec(memory_space=pl.ANY),
        scratch_shapes=[
            pltpu.SMEM((prompts,), jnp.int32),
            pltpu.VMEM(stretch.shape, jnp.bfloat16),
            pltpu.VMEM(stretch.shape, jnp.float32),
            pltpu.VMEM(stretch.shape, jnp.bfloat16),
            pltpu.VMEM((rows, HEAD_SIZE), jnp.bfloat16),
            pltpu.SMEM((groups,), jnp.int32),
            pltpu.SMEM((prompts,), jnp.int32),
            pltpu.SemaphoreType.DMA,
            pltpu.SemaphoreType.DMA((parts,)),
            pltpu.SemaphoreType.DMA,
        ],
        compiler_params=params(PACK_BYTES),
        cost_estimate=cost(0, stretch.size * 2 + groups * CAP * rows * HEAD_SIZE * 2),
        name="pack",
    )(owner, stretch)


def prefill_kernel(pos_ref, query_ref, earlier_ref, stretch_ref, out_ref, split_ref):
    block, earlier_rows, _ = earlier_ref.shape
    fresh_rows = stretch_ref.shape[1]
    prefix, fresh = earlier_rows // 2, fresh_rows // 2
    keys = split_ref.shape[1] // 2
    heads = query_ref.shape[1] // HEAD_SIZE
    step = pl.program_id(0)

    @pl.when(step == 0)
    def _():
        split_ref[...] = jnp.zeros_like(split_ref)

    column = lax.broadcasted_iota(jnp.int32, (fresh, keys), 1)
    row = lax.broadcasted_iota(jnp.int32, (fresh, keys), 0)
    causal = (column >= prefix) & (column - prefix <= row)
    ones = jnp.ones((keys, HEAD_SIZE), jnp.bfloat16)
    for b in range(block):
        split_ref[b, :earlier_rows] = earlier_ref[b].astype(jnp.float32)
        split_ref[b, earlier_rows : earlier_rows + fresh_rows] = stretch_ref[b].astype(jnp.float32)
        key = split_ref[b, pl.ds(0, keys, stride=2), :].astype(jnp.bfloat16)
        value = split_ref[b, pl.ds(1, keys, stride=2), :].astype(jnp.bfloat16)
        value = jnp.concatenate([value, ones], axis=1)
        limit = jnp.minimum(pos_ref[step * block + b], prefix)
        bias = jnp.where((column < limit) | causal, 0.0, MASKED)
        rows = slice(b * fresh, (b + 1) * fresh)
        query = jnp.concatenate(
            [query_ref[rows, h * HEAD_SIZE : (h + 1) * HEAD_SIZE] for h in range(heads)], axis=0
        )
        scores = lax.dot_general(query, key, CONTRACT_LAST, preferred_element_type=jnp.float32)
        scores = scores.reshape(heads, fresh, keys) * SCORE_SCALE + bias[None]
        top = jnp.max(scores, axis=-1, keepdims=True)
        weights = jnp.exp2(scores - top).astype(jnp.bfloat16).reshape(heads * fresh, keys)
        mixed = jnp.dot(weights, value, preferred_element_type=jnp.float32)
        result = (mixed[:, :HEAD_SIZE] / mixed[:, HEAD_SIZE:]).astype(jnp.bfloat16)
        for h in range(heads):
            out_ref[rows, h * HEAD_SIZE : (h + 1) * HEAD_SIZE] = result[
                h * fresh : (h + 1) * fresh
            ]


def prefill(position, query, earlier, stretch):
    prompts, earlier_rows, _ = earlier.shape
    fresh_rows = stretch.shape[1]
    width = query.shape[1]
    block = min(PROMPT_BLOCK, prompts)
    keys = -(-(earlier_rows + fresh_rows) // 2 // 256) * 256
    rows = block * fresh_rows // 2
    return pl.pallas_call(
        prefill_kernel,
        grid=(prompts // block,),
        out_shape=jax.ShapeDtypeStruct(query.shape, jnp.bfloat16),
        in_specs=[
            in_smem(),
            pl.BlockSpec((rows, width), lambda i: (i, 0)),
            pl.BlockSpec((block, earlier_rows, HEAD_SIZE), lambda i: (i, 0, 0)),
            pl.BlockSpec((block, fresh_rows, HEAD_SIZE), lambda i: (i, 0, 0)),
        ],
        out_specs=pl.BlockSpec((rows, width), lambda i: (i, 0)),
        scratch_shapes=[pltpu.VMEM((block, 2 * keys, HEAD_SIZE), jnp.float32)],
        compiler_params=params(),
        cost_estimate=cost(
            query.size * keys * 6,
            (2 * query.size + earlier.size + stretch.size) * 2,
            query.size // HEAD_SIZE * keys,
        ),
        name="prefill",
    )(position, query, earlier, stretch)


def down_kernel(input_ref, weight_ref, adapter_ref, out_ref):
    rows = input_ref.shape[0]
    span = 2 * ADAPTER_RANK
    wide = jnp.dot(input_ref[...], weight_ref[...], preferred_element_type=jnp.float32)
    owner = lax.broadcasted_iota(jnp.int32, wide.shape, 1) // span
    wide = jnp.where(owner == adapter_ref[...], wide, 0.0)
    folded = wide[:, :128] + wide[:, 128:]
    folded = folded + pltpu.roll(folded, 64, 1)
    folded = folded + pltpu.roll(folded, 32, 1)
    out_ref[...] = folded


def down(inputs, weight, adapter):
    rows, width = inputs.shape
    return pl.pallas_call(
        down_kernel,
        out_shape=jax.ShapeDtypeStruct((rows, 128), jnp.float32),
        in_specs=[in_vmem()] * 3,
        out_specs=in_vmem(),
        compiler_params=params(),
        cost_estimate=cost(2 * rows * width * 256, (inputs.size + weight.size) * 2),
        name="adapter_down",
    )(inputs, weight, adapter)


def sum_over_tensor(x):
    count = lax.axis_size("tensor")
    stride = 1
    while stride < count:
        x = x + lax.ppermute(x, "tensor", [(i, i ^ stride) for i in range(count)])
        stride *= 2
    return x


def attend(query, key, value, bias, top, total):
    rows, n = bias.shape
    heads = query.shape[0] // rows
    scores = lax.dot_general(query, key, CONTRACT_LAST, preferred_element_type=jnp.float32)
    scores = (scores.reshape(heads, rows, n) * SCORE_SCALE + bias[None]).reshape(heads * rows, n)
    new_top = jnp.maximum(top, jnp.max(scores, axis=-1, keepdims=True))
    weights = jnp.exp2(scores - new_top).astype(jnp.bfloat16)
    mixed = jnp.dot(weights, value, preferred_element_type=jnp.float32)
    return new_top, total * jnp.exp2(top - new_top) + mixed


def heads_of(ref, first, count):
    return jnp.concatenate(
        [ref[:, h * HEAD_SIZE : (h + 1) * HEAD_SIZE] for h in range(first, first + count)], axis=0
    )


def with_ones(value):
    return jnp.concatenate([value, jnp.ones_like(value)], axis=1)


def page_bias(table_ref, length_ref, page, offset):
    positions = table_ref.shape[1]
    length = length_ref[...]
    last = (length - 1) // PAGE
    times = jnp.zeros((length.shape[0], page.shape[1]), jnp.float32)
    tail_page = jnp.zeros_like(length)
    for p in range(positions):
        named = table_ref[:, p : p + 1]
        times = times + jnp.where(page == jnp.where(last > p, named, -1), 1.0, 0.0)
        tail_page = tail_page + jnp.where(last == p, named, 0)
    in_tail = (page == tail_page) & (offset < length - last * PAGE)
    times = times + jnp.where(in_tail, 1.0, 0.0)
    return jnp.where(times > 0.0, jnp.log2(jnp.maximum(times, 1.0)), MASKED)


def pool_kernel(
    query_ref, pool_ref, table_ref, length_ref, adapter_ref, middle_ref, up_ref, base_ref,
    attended_ref, level_ref, bias_ref, pool_bias_ref, split_ref, base_split_ref,
):
    rows = query_ref.shape[0]
    heads = query_ref.shape[1] // HEAD_SIZE
    pool_tokens = pool_ref.shape[0] // 2
    span = 2 * ADAPTER_RANK
    middle = middle_ref[...]
    middle = jnp.concatenate([middle, middle], axis=1)
    lane = lax.broadcasted_iota(jnp.int32, middle.shape, 1)
    mine = (lane // span) == adapter_ref[...]
    half = (lane % span) // ADAPTER_RANK
    base_split_ref[...] = base_ref[...].astype(jnp.float32)
    fresh = []
    for j in range(2):
        picked = jnp.where(mine & (half == j), middle, 0.0).astype(jnp.bfloat16)
        delta = jnp.dot(picked, up_ref[...], preferred_element_type=jnp.float32)
        base = base_split_ref[pl.ds(j, rows, stride=2), :]
        fresh.append((base + ADAPTER_SCALE * delta).astype(jnp.bfloat16).astype(jnp.float32))
    token = lax.broadcasted_iota(jnp.int32, (1, bias_ref.shape[1]), 1)
    page = (pool_tokens + token) // PAGE
    bias_ref[...] = page_bias(table_ref, length_ref, page, token % PAGE)
    token = lax.broadcasted_iota(jnp.int32, (1, pool_tokens), 1)
    pool_bias_ref[...] = page_bias(table_ref, length_ref, token // PAGE, token % PAGE)
    split_ref[...] = pool_ref[...].astype(jnp.float32)
    key = split_ref[pl.ds(0, pool_tokens, stride=2), :].astype(jnp.bfloat16)
    value = with_ones(split_ref[pl.ds(1, pool_tokens, stride=2), :].astype(jnp.bfloat16))
    own_total = with_ones(fresh[1])
    blocks = 2
    tokens = pool_tokens // blocks
    for first in range(0, heads, HEAD_BLOCK):
        query = heads_of(query_ref, first, HEAD_BLOCK)
        own = query.astype(jnp.float32) * jnp.concatenate([fresh[0]] * HEAD_BLOCK, axis=0)
        top = jnp.sum(own, axis=-1, keepdims=True) * SCORE_SCALE
        total = jnp.concatenate([own_total] * HEAD_BLOCK, axis=0)
        for c in range(blocks):
            block = slice(c * tokens, (c + 1) * tokens)
            top, total = attend(query, key[block], value[block], pool_bias_ref[:, block], top, total)
        attended_ref[first * rows : (first + HEAD_BLOCK) * rows] = total[:, :HEAD_SIZE] / total[:, HEAD_SIZE:]
        level = top + jnp.log2(total[:, HEAD_SIZE : HEAD_SIZE + 1])
        for h in range(HEAD_BLOCK):
            level_ref[:, first + h : first + h + 1] = level[h * rows : (h + 1) * rows]


def pool_decode(query, pool, table, length, adapter, middle, up, base, landing_tokens):
    rows, width = query.shape
    stacked = rows * width // HEAD_SIZE
    pool_tokens = pool.shape[0] // 2
    return pl.pallas_call(
        pool_kernel,
        out_shape=(
            jax.ShapeDtypeStruct((stacked, HEAD_SIZE), jnp.float32),
            jax.ShapeDtypeStruct((rows, stacked // rows), jnp.float32),
            jax.ShapeDtypeStruct((rows, landing_tokens), jnp.float32),
        ),
        in_specs=[in_vmem()] * 8,
        out_specs=[in_vmem()] * 3,
        scratch_shapes=[
            pltpu.VMEM((rows, pool_tokens), jnp.float32),
            pltpu.VMEM(pool.shape, jnp.float32),
            pltpu.VMEM(base.shape, jnp.float32),
        ],
        compiler_params=params(),
        cost_estimate=cost(
            stacked * pool_tokens * HEAD_SIZE * 6, pool.size * 2 + stacked * 1536, stacked * pool_tokens
        ),
        name="pool_decode",
    )(query, pool, table, length, adapter, middle, up, base)


def landing_kernel(query_ref, landing_ref, bias_ref, attended_ref, level_ref, out_ref):
    rows = query_ref.shape[0]
    heads = query_ref.shape[1] // HEAD_SIZE
    groups, cap, slot_rows, _ = landing_ref.shape
    half = slot_rows // 2
    span = min(groups, LANDING_TOKENS // (cap * half))
    tokens = span * cap * half
    for first in range(0, heads, HEAD_BLOCK):
        query = heads_of(query_ref, first, HEAD_BLOCK)
        top = jnp.concatenate(
            [level_ref[:, h : h + 1] for h in range(first, first + HEAD_BLOCK)], axis=0
        )
        total = with_ones(attended_ref[first * rows : (first + HEAD_BLOCK) * rows])
        for c in range(groups // span):
            block = slice(c * span, (c + 1) * span)
            key = landing_ref[block, :, :half].reshape(tokens, HEAD_SIZE)
            value = with_ones(landing_ref[block, :, half:].reshape(tokens, HEAD_SIZE))
            bias = bias_ref[:, c * tokens : (c + 1) * tokens]
            top, total = attend(query, key, value, bias, top, total)
        result = (total[:, :HEAD_SIZE] / total[:, HEAD_SIZE:]).astype(jnp.bfloat16)
        for h in range(HEAD_BLOCK):
            lanes = slice((first + h) * HEAD_SIZE, (first + h + 1) * HEAD_SIZE)
            out_ref[:, lanes] = result[h * rows : (h + 1) * rows]


def landing_decode(query, landing, bias, attended, level):
    stacked = attended.shape[0]
    tokens = bias.shape[1]
    return pl.pallas_call(
        landing_kernel,
        out_shape=jax.ShapeDtypeStruct(query.shape, jnp.bfloat16),
        in_specs=[in_vmem()] * 5,
        out_specs=in_vmem(),
        compiler_params=params(),
        cost_estimate=cost(
            stacked * tokens * HEAD_SIZE * 6, landing.size * 2 + stacked * 1024, stacked * tokens
        ),
        name="landing_decode",
    )(query, landing, bias, attended, level)


def body(
    stretch_query_rows,
    earlier_token_cache,
    stretch_cache,
    stretch_position,
    owning_decode_group,
    decode_query_rows,
    decode_input_rows,
    decode_base_projection,
    row_adapter_index,
    adapter_down_weight,
    adapter_up_weight,
    group_page_store,
    row_page_index,
    cached_token_length,
):
    groups = lax.axis_size("group")
    prompts, stretch_len = stretch_cache.shape[:2]
    prefix_len = earlier_token_cache.shape[1]
    stretch = stretch_cache.reshape(prompts, 2 * stretch_len, HEAD_SIZE)
    earlier = earlier_token_cache.reshape(prompts, 2 * prefix_len, HEAD_SIZE)
    pool = group_page_store.reshape(-1, HEAD_SIZE)
    base = decode_base_projection.reshape(-1, HEAD_SIZE)
    adapter = row_adapter_index[:, None]
    length = cached_token_length[:, None]

    outgoing = pack(owning_decode_group, stretch, groups)
    landing = lax.all_to_all(
        outgoing.reshape(groups, -1, HEAD_SIZE), "group", 0, 0, tiled=True
    ).reshape(outgoing.shape)
    middle = sum_over_tensor(down(decode_input_rows, adapter_down_weight, adapter))
    prefill_out = prefill(stretch_position, stretch_query_rows, earlier, stretch)
    attended, level, bias = pool_decode(
        decode_query_rows, pool, row_page_index, length, adapter, middle, adapter_up_weight, base,
        groups * CAP * stretch_len,
    )
    decode_out = landing_decode(decode_query_rows, landing, bias, attended, level)
    return (prefill_out, decode_out)


def solution(mesh):
    placed = (
        P("group", "tensor"),
        P("group", None, None, "tensor"),
        P("group", None, None, "tensor"),
        P("group"),
        P("group"),
        P("group", "tensor"),
        P("group", "tensor"),
        P("group", None, "tensor"),
        P("group"),
        P("tensor", None),
        P(None, "tensor"),
        P("group", None, None, "tensor"),
        P("group", None),
        P("group"),
    )
    return jax.shard_map(
        body,
        mesh=mesh,
        in_specs=placed,
        out_specs=(P("group", "tensor"), P("group", "tensor")),
        check_vma=False,
    )
```

```python
import functools

import jax
import jax.numpy as jnp
from jax import lax
from jax.experimental import pallas as pl
from jax.experimental.pallas import tpu as pltpu
from jax.sharding import PartitionSpec as P

HEAD_SIZE = 128
ADAPTER_RANK = 16
ADAPTER_COUNT = 8
PAGE = 16
CAP = 2
ADAPTER_SCALE = 2.0
SCORE_SCALE = HEAD_SIZE ** (-0.5) * 1.4426950408889634
MASKED = -1e30
VMEM_BYTES = 24 * 1024 * 1024
PACK_BYTES = 56 * 1024 * 1024
PROMPT_BLOCK = 8
HEAD_BLOCK = 4
LANDING_TOKENS = 768
SAFE_TOTAL = 2.0**100

CONTRACT_LAST = (((1,), (1,)), ((), ()))


def in_vmem():
    return pl.BlockSpec(memory_space=pltpu.VMEM)


def in_smem():
    return pl.BlockSpec(memory_space=pltpu.SMEM)


def params(limit=VMEM_BYTES):
    return pltpu.CompilerParams(vmem_limit_bytes=limit)


def cost(flops, moved, exps=0):
    return pl.CostEstimate(flops=flops, bytes_accessed=moved, transcendentals=exps)


def pack_kernel(
    owner_hbm, kv_hbm, out_hbm, owner_ref, kv_ref, split_ref, stage_ref, zero_ref, count_ref, slot_ref,
    owner_sem, kv_sem, out_sem,
):
    prompts, rows, _ = kv_ref.shape
    tokens = rows // 2
    groups, cap = out_hbm.shape[:2]
    parts = kv_sem.shape[0]
    span = prompts // parts
    owner_copy = pltpu.make_async_copy(owner_hbm, owner_ref, owner_sem)
    owner_copy.start()
    kv_copies = [
        pltpu.make_async_copy(
            kv_hbm.at[pl.ds(c * span, span)], kv_ref.at[pl.ds(c * span, span)], kv_sem.at[c]
        )
        for c in range(parts)
    ]
    for copy in kv_copies:
        copy.start()
    zero_ref[...] = jnp.zeros_like(zero_ref)
    for d in range(groups):
        count_ref[d] = 0
    owner_copy.wait()
    for p in range(prompts):
        dest = owner_ref[p]
        rank = count_ref[dest]
        count_ref[dest] = rank + 1
        slot_ref[p] = jnp.minimum(rank, cap - 1)
    for d in range(groups):
        held = count_ref[d]
        for taken in range(cap):

            @pl.when(held == taken)
            def _():
                rest = pl.ds(0, cap - taken)
                pltpu.make_async_copy(
                    zero_ref.at[rest], out_hbm.at[d, pl.ds(taken, cap - taken)], out_sem
                ).start()

    for c in range(parts):
        kv_copies[c].wait()
        block = slice(c * span, (c + 1) * span)
        split_ref[block] = kv_ref[block].astype(jnp.float32)
        for p in range(c * span, (c + 1) * span):
            for j in range(2):
                part = split_ref[p, pl.ds(j, tokens, stride=2), :]
                stage_ref[p, j * tokens : (j + 1) * tokens] = part.astype(jnp.bfloat16)
        for p in range(c * span, (c + 1) * span):
            pltpu.make_async_copy(
                stage_ref.at[p], out_hbm.at[owner_ref[p], slot_ref[p]], out_sem
            ).start()
    pltpu.make_async_copy(out_hbm, out_hbm, out_sem).wait()


def pack(owner, stretch, groups):
    prompts, rows, _ = stretch.shape
    parts = 4
    return pl.pallas_call(
        pack_kernel,
        out_shape=jax.ShapeDtypeStruct((groups, CAP, rows, HEAD_SIZE), jnp.bfloat16),
        in_specs=[pl.BlockSpec(memory_space=pl.ANY)] * 2,
        out_specs=pl.BlockSpec(memory_space=pl.ANY),
        scratch_shapes=[
            pltpu.SMEM((prompts,), jnp.int32),
            pltpu.VMEM(stretch.shape, jnp.bfloat16),
            pltpu.VMEM(stretch.shape, jnp.float32),
            pltpu.VMEM(stretch.shape, jnp.bfloat16),
            pltpu.VMEM((CAP, rows, HEAD_SIZE), jnp.bfloat16),
            pltpu.SMEM((groups,), jnp.int32),
            pltpu.SMEM((prompts,), jnp.int32),
            pltpu.SemaphoreType.DMA,
            pltpu.SemaphoreType.DMA((parts,)),
            pltpu.SemaphoreType.DMA,
        ],
        compiler_params=params(PACK_BYTES),
        cost_estimate=cost(0, stretch.size * 2 + groups * CAP * rows * HEAD_SIZE * 2),
        name="pack",
    )(owner, stretch)


def prefill_kernel(pos_ref, query_ref, earlier_ref, stretch_ref, out_ref, split_ref):
    block, earlier_rows, _ = earlier_ref.shape
    fresh_rows = stretch_ref.shape[1]
    prefix, fresh = earlier_rows // 2, fresh_rows // 2
    keys = split_ref.shape[1] // 2
    heads = query_ref.shape[1] // HEAD_SIZE
    step = pl.program_id(0)

    @pl.when(step == 0)
    def _():
        split_ref[...] = jnp.zeros_like(split_ref)

    column = lax.broadcasted_iota(jnp.int32, (fresh, keys), 1)
    row = lax.broadcasted_iota(jnp.int32, (fresh, keys), 0)
    causal = (column >= prefix) & (column - prefix <= row)
    ones = jnp.ones((keys, HEAD_SIZE), jnp.bfloat16)
    for b in range(block):
        split_ref[b, :earlier_rows] = earlier_ref[b].astype(jnp.float32)
        split_ref[b, earlier_rows : earlier_rows + fresh_rows] = stretch_ref[b].astype(jnp.float32)
        key = split_ref[b, pl.ds(0, keys, stride=2), :].astype(jnp.bfloat16)
        value = split_ref[b, pl.ds(1, keys, stride=2), :].astype(jnp.bfloat16)
        value = jnp.concatenate([value, ones], axis=1)
        limit = jnp.minimum(pos_ref[step * block + b], prefix)
        bias = jnp.where((column < limit) | causal, 0.0, MASKED)
        rows = slice(b * fresh, (b + 1) * fresh)
        query = jnp.concatenate(
            [query_ref[rows, h * HEAD_SIZE : (h + 1) * HEAD_SIZE] for h in range(heads)], axis=0
        )
        scores = lax.dot_general(query, key, CONTRACT_LAST, preferred_element_type=jnp.float32)
        scores = scores.reshape(heads, fresh, keys) * SCORE_SCALE + bias[None]
        top = jnp.max(scores, axis=-1, keepdims=True)
        weights = jnp.exp2(scores - top).astype(jnp.bfloat16).reshape(heads * fresh, keys)
        mixed = jnp.dot(weights, value, preferred_element_type=jnp.float32)
        result = (mixed[:, :HEAD_SIZE] / mixed[:, HEAD_SIZE:]).astype(jnp.bfloat16)
        for h in range(heads):
            out_ref[rows, h * HEAD_SIZE : (h + 1) * HEAD_SIZE] = result[
                h * fresh : (h + 1) * fresh
            ]


def prefill(position, query, earlier, stretch):
    prompts, earlier_rows, _ = earlier.shape
    fresh_rows = stretch.shape[1]
    width = query.shape[1]
    block = min(PROMPT_BLOCK, prompts)
    keys = -(-(earlier_rows + fresh_rows) // 2 // 256) * 256
    rows = block * fresh_rows // 2
    return pl.pallas_call(
        prefill_kernel,
        grid=(prompts // block,),
        out_shape=jax.ShapeDtypeStruct(query.shape, jnp.bfloat16),
        in_specs=[
            in_smem(),
            pl.BlockSpec((rows, width), lambda i: (i, 0)),
            pl.BlockSpec((block, earlier_rows, HEAD_SIZE), lambda i: (i, 0, 0)),
            pl.BlockSpec((block, fresh_rows, HEAD_SIZE), lambda i: (i, 0, 0)),
        ],
        out_specs=pl.BlockSpec((rows, width), lambda i: (i, 0)),
        scratch_shapes=[pltpu.VMEM((block, 2 * keys, HEAD_SIZE), jnp.float32)],
        compiler_params=params(),
        cost_estimate=cost(
            query.size * keys * 6,
            (2 * query.size + earlier.size + stretch.size) * 2,
            query.size // HEAD_SIZE * keys,
        ),
        name="prefill",
    )(position, query, earlier, stretch)


def down_kernel(input_ref, weight_ref, adapter_ref, out_ref):
    rows = input_ref.shape[0]
    span = 2 * ADAPTER_RANK
    wide = jnp.dot(input_ref[...], weight_ref[...], preferred_element_type=jnp.float32)
    owner = lax.broadcasted_iota(jnp.int32, wide.shape, 1) // span
    wide = jnp.where(owner == adapter_ref[...], wide, 0.0)
    folded = wide[:, :128] + wide[:, 128:]
    folded = folded + pltpu.roll(folded, 64, 1)
    folded = folded + pltpu.roll(folded, 32, 1)
    out_ref[...] = folded


def down(inputs, weight, adapter):
    rows, width = inputs.shape
    return pl.pallas_call(
        down_kernel,
        out_shape=jax.ShapeDtypeStruct((rows, 128), jnp.float32),
        in_specs=[in_vmem()] * 3,
        out_specs=in_vmem(),
        compiler_params=params(),
        cost_estimate=cost(2 * rows * width * 256, (inputs.size + weight.size) * 2),
        name="adapter_down",
    )(inputs, weight, adapter)


def sum_over_tensor(x):
    count = lax.axis_size("tensor")
    stride = 1
    while stride < count:
        x = x + lax.ppermute(x, "tensor", [(i, i ^ stride) for i in range(count)])
        stride *= 2
    return x


def attend(query, key, value, bias, top, total):
    rows, n = bias.shape
    heads = query.shape[0] // rows
    scores = lax.dot_general(query, key, CONTRACT_LAST, preferred_element_type=jnp.float32)
    scores = (scores.reshape(heads, rows, n) * SCORE_SCALE + bias[None]).reshape(heads * rows, n)
    new_top = jnp.maximum(top, jnp.max(scores, axis=-1, keepdims=True))
    weights = jnp.exp2(scores - new_top).astype(jnp.bfloat16)
    mixed = jnp.dot(weights, value, preferred_element_type=jnp.float32)
    return new_top, total * jnp.exp2(top - new_top) + mixed


def heads_of(ref, first, count):
    return jnp.concatenate(
        [ref[:, h * HEAD_SIZE : (h + 1) * HEAD_SIZE] for h in range(first, first + count)], axis=0
    )


def with_ones(value):
    return jnp.concatenate([value, jnp.ones_like(value)], axis=1)


def page_bias(table_ref, length_ref, page, offset):
    positions = table_ref.shape[1]
    length = length_ref[...]
    last = (length - 1) // PAGE
    times = jnp.zeros((length.shape[0], page.shape[1]), jnp.float32)
    tail_page = jnp.zeros_like(length)
    for p in range(positions):
        named = table_ref[:, p : p + 1]
        times = times + jnp.where(page == jnp.where(last > p, named, -1), 1.0, 0.0)
        tail_page = tail_page + jnp.where(last == p, named, 0)
    in_tail = (page == tail_page) & (offset < length - last * PAGE)
    times = times + jnp.where(in_tail, 1.0, 0.0)
    return jnp.where(times > 0.0, jnp.log2(jnp.maximum(times, 1.0)), MASKED)


def pool_kernel(
    query_ref, pool_ref, table_ref, length_ref, adapter_ref, middle_ref, up_ref, base_ref,
    attended_ref, level_ref, bias_ref, pool_bias_ref, split_ref, base_split_ref,
):
    rows = query_ref.shape[0]
    heads = query_ref.shape[1] // HEAD_SIZE
    pool_tokens = pool_ref.shape[0] // 2
    span = 2 * ADAPTER_RANK
    middle = middle_ref[...]
    middle = jnp.concatenate([middle, middle], axis=1)
    lane = lax.broadcasted_iota(jnp.int32, middle.shape, 1)
    mine = (lane // span) == adapter_ref[...]
    half = (lane % span) // ADAPTER_RANK
    base_split_ref[...] = base_ref[...].astype(jnp.float32)
    fresh = []
    for j in range(2):
        picked = jnp.where(mine & (half == j), middle, 0.0).astype(jnp.bfloat16)
        delta = jnp.dot(picked, up_ref[...], preferred_element_type=jnp.float32)
        base = base_split_ref[pl.ds(j, rows, stride=2), :]
        fresh.append((base + ADAPTER_SCALE * delta).astype(jnp.bfloat16).astype(jnp.float32))
    token = lax.broadcasted_iota(jnp.int32, (1, bias_ref.shape[1]), 1)
    page = (pool_tokens + token) // PAGE
    bias_ref[...] = page_bias(table_ref, length_ref, page, token % PAGE)
    token = lax.broadcasted_iota(jnp.int32, (1, pool_tokens), 1)
    pool_bias_ref[...] = page_bias(table_ref, length_ref, token // PAGE, token % PAGE)
    split_ref[...] = pool_ref[...].astype(jnp.float32)
    key = split_ref[pl.ds(0, pool_tokens, stride=2), :].astype(jnp.bfloat16)
    value = with_ones(split_ref[pl.ds(1, pool_tokens, stride=2), :].astype(jnp.bfloat16))
    own_total = with_ones(fresh[1])
    blocks = 2
    tokens = pool_tokens // blocks
    for first in range(0, heads, HEAD_BLOCK):
        query = heads_of(query_ref, first, HEAD_BLOCK)
        own = query.astype(jnp.float32) * jnp.concatenate([fresh[0]] * HEAD_BLOCK, axis=0)
        top = jnp.sum(own, axis=-1, keepdims=True) * SCORE_SCALE
        total = jnp.concatenate([own_total] * HEAD_BLOCK, axis=0)
        for c in range(blocks):
            block = slice(c * tokens, (c + 1) * tokens)
            top, total = attend(query, key[block], value[block], pool_bias_ref[:, block], top, total)
        attended_ref[first * rows : (first + HEAD_BLOCK) * rows] = total[:, :HEAD_SIZE] / total[:, HEAD_SIZE:]
        level = top + jnp.log2(total[:, HEAD_SIZE : HEAD_SIZE + 1])
        for h in range(HEAD_BLOCK):
            level_ref[:, first + h : first + h + 1] = level[h * rows : (h + 1) * rows]


def pool_decode(query, pool, table, length, adapter, middle, up, base, landing_tokens):
    rows, width = query.shape
    stacked = rows * width // HEAD_SIZE
    pool_tokens = pool.shape[0] // 2
    return pl.pallas_call(
        pool_kernel,
        out_shape=(
            jax.ShapeDtypeStruct((stacked, HEAD_SIZE), jnp.float32),
            jax.ShapeDtypeStruct((rows, stacked // rows), jnp.float32),
            jax.ShapeDtypeStruct((rows, landing_tokens), jnp.float32),
        ),
        in_specs=[in_vmem()] * 8,
        out_specs=[in_vmem()] * 3,
        scratch_shapes=[
            pltpu.VMEM((rows, pool_tokens), jnp.float32),
            pltpu.VMEM(pool.shape, jnp.float32),
            pltpu.VMEM(base.shape, jnp.float32),
        ],
        compiler_params=params(),
        cost_estimate=cost(
            stacked * pool_tokens * HEAD_SIZE * 6, pool.size * 2 + stacked * 1536, stacked * pool_tokens
        ),
        name="pool_decode",
    )(query, pool, table, length, adapter, middle, up, base)


def landing_kernel(query_ref, landing_ref, bias_ref, attended_ref, level_ref, out_ref):
    rows = query_ref.shape[0]
    heads = query_ref.shape[1] // HEAD_SIZE
    groups, cap, slot_rows, _ = landing_ref.shape
    half = slot_rows // 2
    span = min(groups, LANDING_TOKENS // (cap * half))
    tokens = span * cap * half

    def begin(first):
        query = heads_of(query_ref, first, HEAD_BLOCK)
        top = jnp.concatenate(
            [level_ref[:, h : h + 1] for h in range(first, first + HEAD_BLOCK)], axis=0
        )
        return query, top, with_ones(attended_ref[first * rows : (first + HEAD_BLOCK) * rows])

    def part(c):
        block = slice(c * span, (c + 1) * span)
        key = landing_ref[block, :, :half].reshape(tokens, HEAD_SIZE)
        value = with_ones(landing_ref[block, :, half:].reshape(tokens, HEAD_SIZE))
        return key, value, bias_ref[:, c * tokens : (c + 1) * tokens]

    def finish(first, total):
        result = (total[:, :HEAD_SIZE] / total[:, HEAD_SIZE:]).astype(jnp.bfloat16)
        for h in range(HEAD_BLOCK):
            lanes = slice((first + h) * HEAD_SIZE, (first + h + 1) * HEAD_SIZE)
            out_ref[:, lanes] = result[h * rows : (h + 1) * rows]

    worst = jnp.zeros((8, HEAD_SIZE), jnp.float32)
    for first in range(0, heads, HEAD_BLOCK):
        query, top, total = begin(first)
        top = top.reshape(HEAD_BLOCK, rows, 1)
        for c in range(groups // span):
            key, value, bias = part(c)
            scores = lax.dot_general(query, key, CONTRACT_LAST, preferred_element_type=jnp.float32)
            scores = scores.reshape(HEAD_BLOCK, rows, tokens) * SCORE_SCALE + (bias[None] - top)
            weights = jnp.exp2(scores).astype(jnp.bfloat16).reshape(HEAD_BLOCK * rows, tokens)
            total = total + jnp.dot(weights, value, preferred_element_type=jnp.float32)
        finish(first, total)
        worst = jnp.maximum(worst, jnp.max(total[:, HEAD_SIZE:].reshape(-1, 8, HEAD_SIZE), axis=0))

    @pl.when(jnp.logical_not(jnp.max(worst) < SAFE_TOTAL))
    def _():
        for first in range(0, heads, HEAD_BLOCK):
            query, top, total = begin(first)
            for c in range(groups // span):
                top, total = attend(query, *part(c), top, total)
            finish(first, total)


def landing_decode(query, landing, bias, attended, level):
    stacked = attended.shape[0]
    tokens = bias.shape[1]
    return pl.pallas_call(
        landing_kernel,
        out_shape=jax.ShapeDtypeStruct(query.shape, jnp.bfloat16),
        in_specs=[in_vmem()] * 5,
        out_specs=in_vmem(),
        compiler_params=params(),
        cost_estimate=cost(
            stacked * tokens * HEAD_SIZE * 6, landing.size * 2 + stacked * 1024, stacked * tokens
        ),
        name="landing_decode",
    )(query, landing, bias, attended, level)


def body(
    stretch_query_rows,
    earlier_token_cache,
    stretch_cache,
    stretch_position,
    owning_decode_group,
    decode_query_rows,
    decode_input_rows,
    decode_base_projection,
    row_adapter_index,
    adapter_down_weight,
    adapter_up_weight,
    group_page_store,
    row_page_index,
    cached_token_length,
):
    groups = lax.axis_size("group")
    prompts, stretch_len = stretch_cache.shape[:2]
    prefix_len = earlier_token_cache.shape[1]
    stretch = stretch_cache.reshape(prompts, 2 * stretch_len, HEAD_SIZE)
    earlier = earlier_token_cache.reshape(prompts, 2 * prefix_len, HEAD_SIZE)
    pool = group_page_store.reshape(-1, HEAD_SIZE)
    base = decode_base_projection.reshape(-1, HEAD_SIZE)
    adapter = row_adapter_index[:, None]
    length = cached_token_length[:, None]

    outgoing = pack(owning_decode_group, stretch, groups)
    landing = lax.all_to_all(
        outgoing.reshape(groups, -1, HEAD_SIZE), "group", 0, 0, tiled=True
    ).reshape(outgoing.shape)
    middle = sum_over_tensor(down(decode_input_rows, adapter_down_weight, adapter))
    prefill_out = prefill(stretch_position, stretch_query_rows, earlier, stretch)
    attended, level, bias = pool_decode(
        decode_query_rows, pool, row_page_index, length, adapter, middle, adapter_up_weight, base,
        groups * CAP * stretch_len,
    )
    decode_out = landing_decode(decode_query_rows, landing, bias, attended, level)
    return (prefill_out, decode_out)


def solution(mesh):
    placed = (
        P("group", "tensor"),
        P("group", None, None, "tensor"),
        P("group", None, None, "tensor"),
        P("group"),
        P("group"),
        P("group", "tensor"),
        P("group", "tensor"),
        P("group", None, "tensor"),
        P("group"),
        P("tensor", None),
        P(None, "tensor"),
        P("group", None, None, "tensor"),
        P("group", None),
        P("group"),
    )
    return jax.shard_map(
        body,
        mesh=mesh,
        in_specs=placed,
        out_specs=(P("group", "tensor"), P("group", "tensor")),
        check_vma=False,
    )
```

```python
import functools

import jax
import jax.numpy as jnp
from jax import lax
from jax.experimental import pallas as pl
from jax.experimental.pallas import tpu as pltpu
from jax.sharding import PartitionSpec as P

HEAD_SIZE = 128
ADAPTER_RANK = 16
ADAPTER_COUNT = 8
PAGE = 16
CAP = 2
ADAPTER_SCALE = 2.0
SCORE_SCALE = HEAD_SIZE ** (-0.5) * 1.4426950408889634
MASKED = -1e30
VMEM_BYTES = 24 * 1024 * 1024
PACK_BYTES = 56 * 1024 * 1024
PROMPT_BLOCK = 8
HEAD_BLOCK = 2
LANDING_TOKENS = 768
SAFE_TOTAL = 2.0**100

CONTRACT_LAST = (((1,), (1,)), ((), ()))


def in_vmem():
    return pl.BlockSpec(memory_space=pltpu.VMEM)


def in_smem():
    return pl.BlockSpec(memory_space=pltpu.SMEM)


def params(limit=VMEM_BYTES):
    return pltpu.CompilerParams(vmem_limit_bytes=limit)


def cost(flops, moved, exps=0):
    return pl.CostEstimate(flops=flops, bytes_accessed=moved, transcendentals=exps)


def pack_kernel(
    owner_hbm, kv_hbm, out_hbm, owner_ref, kv_ref, split_ref, stage_ref, zero_ref, count_ref, slot_ref,
    owner_sem, kv_sem, out_sem,
):
    prompts, rows, _ = kv_ref.shape
    tokens = rows // 2
    groups, cap = out_hbm.shape[:2]
    parts = kv_sem.shape[0]
    span = prompts // parts
    owner_copy = pltpu.make_async_copy(owner_hbm, owner_ref, owner_sem)
    owner_copy.start()
    kv_copies = [
        pltpu.make_async_copy(
            kv_hbm.at[pl.ds(c * span, span)], kv_ref.at[pl.ds(c * span, span)], kv_sem.at[c]
        )
        for c in range(parts)
    ]
    for copy in kv_copies:
        copy.start()
    zero_ref[...] = jnp.zeros_like(zero_ref)
    for d in range(groups):
        count_ref[d] = 0
    owner_copy.wait()
    for p in range(prompts):
        dest = owner_ref[p]
        rank = count_ref[dest]
        count_ref[dest] = rank + 1
        slot_ref[p] = jnp.minimum(rank, cap - 1)
    for d in range(groups):
        held = count_ref[d]
        for taken in range(cap):

            @pl.when(held == taken)
            def _():
                rest = pl.ds(0, cap - taken)
                pltpu.make_async_copy(
                    zero_ref.at[rest], out_hbm.at[d, pl.ds(taken, cap - taken)], out_sem
                ).start()

    for c in range(parts):
        kv_copies[c].wait()
        block = slice(c * span, (c + 1) * span)
        split_ref[block] = kv_ref[block].astype(jnp.float32)
        for p in range(c * span, (c + 1) * span):
            for j in range(2):
                part = split_ref[p, pl.ds(j, tokens, stride=2), :]
                stage_ref[p, j * tokens : (j + 1) * tokens] = part.astype(jnp.bfloat16)
        for p in range(c * span, (c + 1) * span):
            pltpu.make_async_copy(
                stage_ref.at[p], out_hbm.at[owner_ref[p], slot_ref[p]], out_sem
            ).start()
    pltpu.make_async_copy(out_hbm, out_hbm, out_sem).wait()


def pack(owner, stretch, groups):
    prompts, rows, _ = stretch.shape
    parts = 4
    return pl.pallas_call(
        pack_kernel,
        out_shape=jax.ShapeDtypeStruct((groups, CAP, rows, HEAD_SIZE), jnp.bfloat16),
        in_specs=[pl.BlockSpec(memory_space=pl.ANY)] * 2,
        out_specs=pl.BlockSpec(memory_space=pl.ANY),
        scratch_shapes=[
            pltpu.SMEM((prompts,), jnp.int32),
            pltpu.VMEM(stretch.shape, jnp.bfloat16),
            pltpu.VMEM(stretch.shape, jnp.float32),
            pltpu.VMEM(stretch.shape, jnp.bfloat16),
            pltpu.VMEM((CAP, rows, HEAD_SIZE), jnp.bfloat16),
            pltpu.SMEM((groups,), jnp.int32),
            pltpu.SMEM((prompts,), jnp.int32),
            pltpu.SemaphoreType.DMA,
            pltpu.SemaphoreType.DMA((parts,)),
            pltpu.SemaphoreType.DMA,
        ],
        compiler_params=params(PACK_BYTES),
        cost_estimate=cost(0, stretch.size * 2 + groups * CAP * rows * HEAD_SIZE * 2),
        name="pack",
    )(owner, stretch)


def prefill_kernel(pos_ref, query_ref, earlier_ref, stretch_ref, out_ref, split_ref):
    block, earlier_rows, _ = earlier_ref.shape
    fresh_rows = stretch_ref.shape[1]
    prefix, fresh = earlier_rows // 2, fresh_rows // 2
    keys = split_ref.shape[1] // 2
    heads = query_ref.shape[1] // HEAD_SIZE
    step = pl.program_id(0)

    @pl.when(step == 0)
    def _():
        split_ref[...] = jnp.zeros_like(split_ref)

    column = lax.broadcasted_iota(jnp.int32, (fresh, keys), 1)
    row = lax.broadcasted_iota(jnp.int32, (fresh, keys), 0)
    causal = (column >= prefix) & (column - prefix <= row)
    ones = jnp.ones((keys, HEAD_SIZE), jnp.bfloat16)
    for b in range(block):
        split_ref[b, :earlier_rows] = earlier_ref[b].astype(jnp.float32)
        split_ref[b, earlier_rows : earlier_rows + fresh_rows] = stretch_ref[b].astype(jnp.float32)
        key = split_ref[b, pl.ds(0, keys, stride=2), :].astype(jnp.bfloat16)
        value = split_ref[b, pl.ds(1, keys, stride=2), :].astype(jnp.bfloat16)
        value = jnp.concatenate([value, ones], axis=1)
        limit = jnp.minimum(pos_ref[step * block + b], prefix)
        bias = jnp.where((column < limit) | causal, 0.0, MASKED)
        rows = slice(b * fresh, (b + 1) * fresh)
        query = jnp.concatenate(
            [query_ref[rows, h * HEAD_SIZE : (h + 1) * HEAD_SIZE] for h in range(heads)], axis=0
        )
        scores = lax.dot_general(query, key, CONTRACT_LAST, preferred_element_type=jnp.float32)
        scores = scores.reshape(heads, fresh, keys) * SCORE_SCALE + bias[None]
        top = jnp.max(scores, axis=-1, keepdims=True)
        weights = jnp.exp2(scores - top).astype(jnp.bfloat16).reshape(heads * fresh, keys)
        mixed = jnp.dot(weights, value, preferred_element_type=jnp.float32)
        result = (mixed[:, :HEAD_SIZE] / mixed[:, HEAD_SIZE:]).astype(jnp.bfloat16)
        for h in range(heads):
            out_ref[rows, h * HEAD_SIZE : (h + 1) * HEAD_SIZE] = result[
                h * fresh : (h + 1) * fresh
            ]


def prefill(position, query, earlier, stretch):
    prompts, earlier_rows, _ = earlier.shape
    fresh_rows = stretch.shape[1]
    width = query.shape[1]
    block = min(PROMPT_BLOCK, prompts)
    keys = -(-(earlier_rows + fresh_rows) // 2 // 256) * 256
    rows = block * fresh_rows // 2
    return pl.pallas_call(
        prefill_kernel,
        grid=(prompts // block,),
        out_shape=jax.ShapeDtypeStruct(query.shape, jnp.bfloat16),
        in_specs=[
            in_smem(),
            pl.BlockSpec((rows, width), lambda i: (i, 0)),
            pl.BlockSpec((block, earlier_rows, HEAD_SIZE), lambda i: (i, 0, 0)),
            pl.BlockSpec((block, fresh_rows, HEAD_SIZE), lambda i: (i, 0, 0)),
        ],
        out_specs=pl.BlockSpec((rows, width), lambda i: (i, 0)),
        scratch_shapes=[pltpu.VMEM((block, 2 * keys, HEAD_SIZE), jnp.float32)],
        compiler_params=params(),
        cost_estimate=cost(
            query.size * keys * 6,
            (2 * query.size + earlier.size + stretch.size) * 2,
            query.size // HEAD_SIZE * keys,
        ),
        name="prefill",
    )(position, query, earlier, stretch)


def down_kernel(input_ref, weight_ref, adapter_ref, out_ref):
    rows = input_ref.shape[0]
    span = 2 * ADAPTER_RANK
    wide = jnp.dot(input_ref[...], weight_ref[...], preferred_element_type=jnp.float32)
    owner = lax.broadcasted_iota(jnp.int32, wide.shape, 1) // span
    wide = jnp.where(owner == adapter_ref[...], wide, 0.0)
    folded = wide[:, :128] + wide[:, 128:]
    folded = folded + pltpu.roll(folded, 64, 1)
    folded = folded + pltpu.roll(folded, 32, 1)
    out_ref[...] = folded


def down(inputs, weight, adapter):
    rows, width = inputs.shape
    return pl.pallas_call(
        down_kernel,
        out_shape=jax.ShapeDtypeStruct((rows, 128), jnp.float32),
        in_specs=[in_vmem()] * 3,
        out_specs=in_vmem(),
        compiler_params=params(),
        cost_estimate=cost(2 * rows * width * 256, (inputs.size + weight.size) * 2),
        name="adapter_down",
    )(inputs, weight, adapter)


def sum_over_tensor(x):
    count = lax.axis_size("tensor")
    stride = 1
    while stride < count:
        x = x + lax.ppermute(x, "tensor", [(i, i ^ stride) for i in range(count)])
        stride *= 2
    return x


def attend(query, key, value, bias, top, total):
    rows, n = bias.shape
    heads = query.shape[0] // rows
    scores = lax.dot_general(query, key, CONTRACT_LAST, preferred_element_type=jnp.float32)
    scores = (scores.reshape(heads, rows, n) * SCORE_SCALE + bias[None]).reshape(heads * rows, n)
    new_top = jnp.maximum(top, jnp.max(scores, axis=-1, keepdims=True))
    weights = jnp.exp2(scores - new_top).astype(jnp.bfloat16)
    mixed = jnp.dot(weights, value, preferred_element_type=jnp.float32)
    return new_top, total * jnp.exp2(top - new_top) + mixed


def heads_of(ref, first, count):
    return jnp.concatenate(
        [ref[:, h * HEAD_SIZE : (h + 1) * HEAD_SIZE] for h in range(first, first + count)], axis=0
    )


def with_ones(value):
    return jnp.concatenate([value, jnp.ones_like(value)], axis=1)


def page_bias(table_ref, length_ref, page, offset):
    positions = table_ref.shape[1]
    length = length_ref[...]
    last = (length - 1) // PAGE
    times = jnp.zeros((length.shape[0], page.shape[1]), jnp.float32)
    tail_page = jnp.zeros_like(length)
    for p in range(positions):
        named = table_ref[:, p : p + 1]
        times = times + jnp.where(page == jnp.where(last > p, named, -1), 1.0, 0.0)
        tail_page = tail_page + jnp.where(last == p, named, 0)
    in_tail = (page == tail_page) & (offset < length - last * PAGE)
    times = times + jnp.where(in_tail, 1.0, 0.0)
    return jnp.where(times > 0.0, jnp.log2(jnp.maximum(times, 1.0)), MASKED)


def pool_kernel(
    query_ref, pool_ref, table_ref, length_ref, adapter_ref, middle_ref, up_ref, base_ref,
    attended_ref, level_ref, bias_ref, pool_bias_ref, split_ref, base_split_ref,
):
    rows = query_ref.shape[0]
    heads = query_ref.shape[1] // HEAD_SIZE
    pool_tokens = pool_ref.shape[0] // 2
    span = 2 * ADAPTER_RANK
    middle = middle_ref[...]
    middle = jnp.concatenate([middle, middle], axis=1)
    lane = lax.broadcasted_iota(jnp.int32, middle.shape, 1)
    mine = (lane // span) == adapter_ref[...]
    half = (lane % span) // ADAPTER_RANK
    base_split_ref[...] = base_ref[...].astype(jnp.float32)
    fresh = []
    for j in range(2):
        picked = jnp.where(mine & (half == j), middle, 0.0).astype(jnp.bfloat16)
        delta = jnp.dot(picked, up_ref[...], preferred_element_type=jnp.float32)
        base = base_split_ref[pl.ds(j, rows, stride=2), :]
        fresh.append((base + ADAPTER_SCALE * delta).astype(jnp.bfloat16).astype(jnp.float32))
    token = lax.broadcasted_iota(jnp.int32, (1, bias_ref.shape[1]), 1)
    page = (pool_tokens + token) // PAGE
    bias_ref[...] = page_bias(table_ref, length_ref, page, token % PAGE)
    token = lax.broadcasted_iota(jnp.int32, (1, pool_tokens), 1)
    pool_bias_ref[...] = page_bias(table_ref, length_ref, token // PAGE, token % PAGE)
    split_ref[...] = pool_ref[...].astype(jnp.float32)
    key = split_ref[pl.ds(0, pool_tokens, stride=2), :].astype(jnp.bfloat16)
    value = with_ones(split_ref[pl.ds(1, pool_tokens, stride=2), :].astype(jnp.bfloat16))
    own_total = with_ones(fresh[1])
    blocks = 2
    tokens = pool_tokens // blocks
    for first in range(0, heads, HEAD_BLOCK):
        query = heads_of(query_ref, first, HEAD_BLOCK)
        own = query.astype(jnp.float32) * jnp.concatenate([fresh[0]] * HEAD_BLOCK, axis=0)
        top = jnp.sum(own, axis=-1, keepdims=True) * SCORE_SCALE
        total = jnp.concatenate([own_total] * HEAD_BLOCK, axis=0)
        for c in range(blocks):
            block = slice(c * tokens, (c + 1) * tokens)
            top, total = attend(query, key[block], value[block], pool_bias_ref[:, block], top, total)
        attended_ref[first * rows : (first + HEAD_BLOCK) * rows] = total[:, :HEAD_SIZE] / total[:, HEAD_SIZE:]
        level = top + jnp.log2(total[:, HEAD_SIZE : HEAD_SIZE + 1])
        for h in range(HEAD_BLOCK):
            level_ref[:, first + h : first + h + 1] = level[h * rows : (h + 1) * rows]


def pool_decode(query, pool, table, length, adapter, middle, up, base, landing_tokens):
    rows, width = query.shape
    stacked = rows * width // HEAD_SIZE
    pool_tokens = pool.shape[0] // 2
    return pl.pallas_call(
        pool_kernel,
        out_shape=(
            jax.ShapeDtypeStruct((stacked, HEAD_SIZE), jnp.float32),
            jax.ShapeDtypeStruct((rows, stacked // rows), jnp.float32),
            jax.ShapeDtypeStruct((rows, landing_tokens), jnp.float32),
        ),
        in_specs=[in_vmem()] * 8,
        out_specs=[in_vmem()] * 3,
        scratch_shapes=[
            pltpu.VMEM((rows, pool_tokens), jnp.float32),
            pltpu.VMEM(pool.shape, jnp.float32),
            pltpu.VMEM(base.shape, jnp.float32),
        ],
        compiler_params=params(),
        cost_estimate=cost(
            stacked * pool_tokens * HEAD_SIZE * 6, pool.size * 2 + stacked * 1536, stacked * pool_tokens
        ),
        name="pool_decode",
    )(query, pool, table, length, adapter, middle, up, base)


def landing_kernel(query_ref, landing_ref, bias_ref, attended_ref, level_ref, out_hbm, out_ref, out_sem):
    rows = query_ref.shape[0]
    heads = query_ref.shape[1] // HEAD_SIZE
    groups, cap, slot_rows, _ = landing_ref.shape
    half = slot_rows // 2
    span = min(groups, LANDING_TOKENS // (cap * half))
    tokens = span * cap * half

    def begin(first):
        query = heads_of(query_ref, first, HEAD_BLOCK)
        top = jnp.concatenate(
            [level_ref[:, h : h + 1] for h in range(first, first + HEAD_BLOCK)], axis=0
        )
        return query, top, with_ones(attended_ref[first * rows : (first + HEAD_BLOCK) * rows])

    def part(c):
        block = slice(c * span, (c + 1) * span)
        key = landing_ref[block, :, :half].reshape(tokens, HEAD_SIZE)
        value = with_ones(landing_ref[block, :, half:].reshape(tokens, HEAD_SIZE))
        return key, value, bias_ref[:, c * tokens : (c + 1) * tokens]

    def finish(first, total):
        result = (total[:, :HEAD_SIZE] / total[:, HEAD_SIZE:]).astype(jnp.bfloat16)
        for h in range(HEAD_BLOCK):
            lanes = slice((first + h) * HEAD_SIZE, (first + h + 1) * HEAD_SIZE)
            out_ref[:, lanes] = result[h * rows : (h + 1) * rows]

    def leave(first):
        lanes = pl.ds(first * HEAD_SIZE, HEAD_BLOCK * HEAD_SIZE)
        return pltpu.make_async_copy(
            out_ref.at[:, lanes], out_hbm.at[:, lanes], out_sem.at[first // HEAD_BLOCK]
        )

    worst = jnp.zeros((8, HEAD_SIZE), jnp.float32)
    for first in range(0, heads, HEAD_BLOCK):
        query, top, total = begin(first)
        top = top.reshape(HEAD_BLOCK, rows, 1)
        for c in range(groups // span):
            key, value, bias = part(c)
            scores = lax.dot_general(query, key, CONTRACT_LAST, preferred_element_type=jnp.float32)
            scores = scores.reshape(HEAD_BLOCK, rows, tokens) * SCORE_SCALE + (bias[None] - top)
            weights = jnp.exp2(scores).astype(jnp.bfloat16).reshape(HEAD_BLOCK * rows, tokens)
            total = total + jnp.dot(weights, value, preferred_element_type=jnp.float32)
        finish(first, total)
        leave(first).start()
        worst = jnp.maximum(worst, jnp.max(total[:, HEAD_SIZE:].reshape(-1, 8, HEAD_SIZE), axis=0))

    for first in range(0, heads, HEAD_BLOCK):
        leave(first).wait()

    @pl.when(jnp.logical_not(jnp.max(worst) < SAFE_TOTAL))
    def _():
        for first in range(0, heads, HEAD_BLOCK):
            query, top, total = begin(first)
            for c in range(groups // span):
                top, total = attend(query, *part(c), top, total)
            finish(first, total)
            leave(first).start()
            leave(first).wait()


def landing_decode(query, landing, bias, attended, level):
    stacked = attended.shape[0]
    tokens = bias.shape[1]
    return pl.pallas_call(
        landing_kernel,
        out_shape=jax.ShapeDtypeStruct(query.shape, jnp.bfloat16),
        in_specs=[in_vmem()] * 5,
        out_specs=pl.BlockSpec(memory_space=pl.ANY),
        scratch_shapes=[
            pltpu.VMEM(query.shape, query.dtype),
            pltpu.SemaphoreType.DMA((query.shape[1] // (HEAD_BLOCK * HEAD_SIZE),)),
        ],
        compiler_params=params(),
        cost_estimate=cost(
            stacked * tokens * HEAD_SIZE * 6, landing.size * 2 + stacked * 1024, stacked * tokens
        ),
        name="landing_decode",
    )(query, landing, bias, attended, level)


def body(
    stretch_query_rows,
    earlier_token_cache,
    stretch_cache,
    stretch_position,
    owning_decode_group,
    decode_query_rows,
    decode_input_rows,
    decode_base_projection,
    row_adapter_index,
    adapter_down_weight,
    adapter_up_weight,
    group_page_store,
    row_page_index,
    cached_token_length,
):
    groups = lax.axis_size("group")
    prompts, stretch_len = stretch_cache.shape[:2]
    prefix_len = earlier_token_cache.shape[1]
    stretch = stretch_cache.reshape(prompts, 2 * stretch_len, HEAD_SIZE)
    earlier = earlier_token_cache.reshape(prompts, 2 * prefix_len, HEAD_SIZE)
    pool = group_page_store.reshape(-1, HEAD_SIZE)
    base = decode_base_projection.reshape(-1, HEAD_SIZE)
    adapter = row_adapter_index[:, None]
    length = cached_token_length[:, None]

    outgoing = pack(owning_decode_group, stretch, groups)
    landing = lax.all_to_all(
        outgoing.reshape(groups, -1, HEAD_SIZE), "group", 0, 0, tiled=True
    ).reshape(outgoing.shape)
    middle = sum_over_tensor(down(decode_input_rows, adapter_down_weight, adapter))
    prefill_out = prefill(stretch_position, stretch_query_rows, earlier, stretch)
    attended, level, bias = pool_decode(
        decode_query_rows, pool, row_page_index, length, adapter, middle, adapter_up_weight, base,
        groups * CAP * stretch_len,
    )
    decode_out = landing_decode(decode_query_rows, landing, bias, attended, level)
    return (prefill_out, decode_out)


def solution(mesh):
    placed = (
        P("group", "tensor"),
        P("group", None, None, "tensor"),
        P("group", None, None, "tensor"),
        P("group"),
        P("group"),
        P("group", "tensor"),
        P("group", "tensor"),
        P("group", None, "tensor"),
        P("group"),
        P("tensor", None),
        P(None, "tensor"),
        P("group", None, None, "tensor"),
        P("group", None),
        P("group"),
    )
    return jax.shard_map(
        body,
        mesh=mesh,
        in_specs=placed,
        out_specs=(P("group", "tensor"), P("group", "tensor")),
        check_vma=False,
    )
```

```python
import functools

import jax
import jax.numpy as jnp
from jax import lax
from jax.experimental import pallas as pl
from jax.experimental.pallas import tpu as pltpu
from jax.sharding import PartitionSpec as P

HEAD_SIZE = 128
ADAPTER_RANK = 16
ADAPTER_COUNT = 8
PAGE = 16
CAP = 2
ADAPTER_SCALE = 2.0
SCORE_SCALE = HEAD_SIZE ** (-0.5) * 1.4426950408889634
MASKED = -1e30
VMEM_BYTES = 24 * 1024 * 1024
PACK_BYTES = 56 * 1024 * 1024
PROMPT_BLOCK = 8
HEAD_BLOCK = 2
LANDING_TOKENS = 768
SAFE_TOTAL = 2.0**100

CONTRACT_LAST = (((1,), (1,)), ((), ()))


def in_vmem():
    return pl.BlockSpec(memory_space=pltpu.VMEM)


def in_smem():
    return pl.BlockSpec(memory_space=pltpu.SMEM)


def params(limit=VMEM_BYTES):
    return pltpu.CompilerParams(vmem_limit_bytes=limit)


def cost(flops, moved, exps=0):
    return pl.CostEstimate(flops=flops, bytes_accessed=moved, transcendentals=exps)


def pack_kernel(
    owner_hbm, kv_hbm, out_hbm, owner_ref, kv_ref, split_ref, stage_ref, zero_ref, count_ref, slot_ref,
    owner_sem, kv_sem, out_sem,
):
    prompts, rows, _ = kv_ref.shape
    tokens = rows // 2
    groups, cap = out_hbm.shape[:2]
    parts = kv_sem.shape[0]
    span = prompts // parts
    owner_copy = pltpu.make_async_copy(owner_hbm, owner_ref, owner_sem)
    owner_copy.start()
    kv_copies = [
        pltpu.make_async_copy(
            kv_hbm.at[pl.ds(c * span, span)], kv_ref.at[pl.ds(c * span, span)], kv_sem.at[c]
        )
        for c in range(parts)
    ]
    for copy in kv_copies:
        copy.start()
    zero_ref[...] = jnp.zeros_like(zero_ref)
    for d in range(groups):
        count_ref[d] = 0
    owner_copy.wait()
    for p in range(prompts):
        dest = owner_ref[p]
        rank = count_ref[dest]
        count_ref[dest] = rank + 1
        slot_ref[p] = jnp.minimum(rank, cap - 1)
    for d in range(groups):
        held = count_ref[d]
        for taken in range(cap):

            @pl.when(held == taken)
            def _():
                rest = pl.ds(0, cap - taken)
                pltpu.make_async_copy(
                    zero_ref.at[rest], out_hbm.at[d, pl.ds(taken, cap - taken)], out_sem
                ).start()

    for c in range(parts):
        kv_copies[c].wait()
        block = slice(c * span, (c + 1) * span)
        split_ref[block] = kv_ref[block].astype(jnp.float32)
        for p in range(c * span, (c + 1) * span):
            for j in range(2):
                part = split_ref[p, pl.ds(j, tokens, stride=2), :]
                stage_ref[p, j * tokens : (j + 1) * tokens] = part.astype(jnp.bfloat16)
        for p in range(c * span, (c + 1) * span):
            pltpu.make_async_copy(
                stage_ref.at[p], out_hbm.at[owner_ref[p], slot_ref[p]], out_sem
            ).start()
    pltpu.make_async_copy(out_hbm, out_hbm, out_sem).wait()


def pack(owner, stretch, groups):
    prompts, rows, _ = stretch.shape
    parts = 8
    return pl.pallas_call(
        pack_kernel,
        out_shape=jax.ShapeDtypeStruct((groups, CAP, rows, HEAD_SIZE), jnp.bfloat16),
        in_specs=[pl.BlockSpec(memory_space=pl.ANY)] * 2,
        out_specs=pl.BlockSpec(memory_space=pl.ANY),
        scratch_shapes=[
            pltpu.SMEM((prompts,), jnp.int32),
            pltpu.VMEM(stretch.shape, jnp.bfloat16),
            pltpu.VMEM(stretch.shape, jnp.float32),
            pltpu.VMEM(stretch.shape, jnp.bfloat16),
            pltpu.VMEM((CAP, rows, HEAD_SIZE), jnp.bfloat16),
            pltpu.SMEM((groups,), jnp.int32),
            pltpu.SMEM((prompts,), jnp.int32),
            pltpu.SemaphoreType.DMA,
            pltpu.SemaphoreType.DMA((parts,)),
            pltpu.SemaphoreType.DMA,
        ],
        compiler_params=params(PACK_BYTES),
        cost_estimate=cost(0, stretch.size * 2 + groups * CAP * rows * HEAD_SIZE * 2),
        name="pack",
    )(owner, stretch)


def prefill_kernel(pos_ref, query_ref, earlier_ref, stretch_ref, out_ref, split_ref):
    block, earlier_rows, _ = earlier_ref.shape
    fresh_rows = stretch_ref.shape[1]
    prefix, fresh = earlier_rows // 2, fresh_rows // 2
    keys = split_ref.shape[1] // 2
    heads = query_ref.shape[1] // HEAD_SIZE
    step = pl.program_id(0)

    @pl.when(step == 0)
    def _():
        split_ref[...] = jnp.zeros_like(split_ref)

    column = lax.broadcasted_iota(jnp.int32, (fresh, keys), 1)
    row = lax.broadcasted_iota(jnp.int32, (fresh, keys), 0)
    causal = (column >= prefix) & (column - prefix <= row)
    ones = jnp.ones((keys, HEAD_SIZE), jnp.bfloat16)
    for b in range(block):
        split_ref[b, :earlier_rows] = earlier_ref[b].astype(jnp.float32)
        split_ref[b, earlier_rows : earlier_rows + fresh_rows] = stretch_ref[b].astype(jnp.float32)
        key = split_ref[b, pl.ds(0, keys, stride=2), :].astype(jnp.bfloat16)
        value = split_ref[b, pl.ds(1, keys, stride=2), :].astype(jnp.bfloat16)
        value = jnp.concatenate([value, ones], axis=1)
        limit = jnp.minimum(pos_ref[step * block + b], prefix)
        bias = jnp.where((column < limit) | causal, 0.0, MASKED)
        rows = slice(b * fresh, (b + 1) * fresh)
        query = jnp.concatenate(
            [query_ref[rows, h * HEAD_SIZE : (h + 1) * HEAD_SIZE] for h in range(heads)], axis=0
        )
        scores = lax.dot_general(query, key, CONTRACT_LAST, preferred_element_type=jnp.float32)
        scores = scores.reshape(heads, fresh, keys) * SCORE_SCALE + bias[None]
        top = jnp.max(scores, axis=-1, keepdims=True)
        weights = jnp.exp2(scores - top).astype(jnp.bfloat16).reshape(heads * fresh, keys)
        mixed = jnp.dot(weights, value, preferred_element_type=jnp.float32)
        result = (mixed[:, :HEAD_SIZE] / mixed[:, HEAD_SIZE:]).astype(jnp.bfloat16)
        for h in range(heads):
            out_ref[rows, h * HEAD_SIZE : (h + 1) * HEAD_SIZE] = result[
                h * fresh : (h + 1) * fresh
            ]


def prefill(position, query, earlier, stretch):
    prompts, earlier_rows, _ = earlier.shape
    fresh_rows = stretch.shape[1]
    width = query.shape[1]
    block = min(PROMPT_BLOCK, prompts)
    keys = -(-(earlier_rows + fresh_rows) // 2 // 256) * 256
    rows = block * fresh_rows // 2
    return pl.pallas_call(
        prefill_kernel,
        grid=(prompts // block,),
        out_shape=jax.ShapeDtypeStruct(query.shape, jnp.bfloat16),
        in_specs=[
            in_smem(),
            pl.BlockSpec((rows, width), lambda i: (i, 0)),
            pl.BlockSpec((block, earlier_rows, HEAD_SIZE), lambda i: (i, 0, 0)),
            pl.BlockSpec((block, fresh_rows, HEAD_SIZE), lambda i: (i, 0, 0)),
        ],
        out_specs=pl.BlockSpec((rows, width), lambda i: (i, 0)),
        scratch_shapes=[pltpu.VMEM((block, 2 * keys, HEAD_SIZE), jnp.float32)],
        compiler_params=params(),
        cost_estimate=cost(
            query.size * keys * 6,
            (2 * query.size + earlier.size + stretch.size) * 2,
            query.size // HEAD_SIZE * keys,
        ),
        name="prefill",
    )(position, query, earlier, stretch)


def down_kernel(input_ref, weight_ref, adapter_ref, out_ref):
    rows = input_ref.shape[0]
    span = 2 * ADAPTER_RANK
    wide = jnp.dot(input_ref[...], weight_ref[...], preferred_element_type=jnp.float32)
    owner = lax.broadcasted_iota(jnp.int32, wide.shape, 1) // span
    wide = jnp.where(owner == adapter_ref[...], wide, 0.0)
    folded = wide[:, :128] + wide[:, 128:]
    folded = folded + pltpu.roll(folded, 64, 1)
    folded = folded + pltpu.roll(folded, 32, 1)
    out_ref[...] = folded


def down(inputs, weight, adapter):
    rows, width = inputs.shape
    return pl.pallas_call(
        down_kernel,
        out_shape=jax.ShapeDtypeStruct((rows, 128), jnp.float32),
        in_specs=[in_vmem()] * 3,
        out_specs=in_vmem(),
        compiler_params=params(),
        cost_estimate=cost(2 * rows * width * 256, (inputs.size + weight.size) * 2),
        name="adapter_down",
    )(inputs, weight, adapter)


def sum_over_tensor(x):
    count = lax.axis_size("tensor")
    stride = 1
    while stride < count:
        x = x + lax.ppermute(x, "tensor", [(i, i ^ stride) for i in range(count)])
        stride *= 2
    return x


def attend(query, key, value, bias, top, total):
    rows, n = bias.shape
    heads = query.shape[0] // rows
    scores = lax.dot_general(query, key, CONTRACT_LAST, preferred_element_type=jnp.float32)
    scores = (scores.reshape(heads, rows, n) * SCORE_SCALE + bias[None]).reshape(heads * rows, n)
    new_top = jnp.maximum(top, jnp.max(scores, axis=-1, keepdims=True))
    weights = jnp.exp2(scores - new_top).astype(jnp.bfloat16)
    mixed = jnp.dot(weights, value, preferred_element_type=jnp.float32)
    return new_top, total * jnp.exp2(top - new_top) + mixed


def heads_of(ref, first, count):
    return jnp.concatenate(
        [ref[:, h * HEAD_SIZE : (h + 1) * HEAD_SIZE] for h in range(first, first + count)], axis=0
    )


def with_ones(value):
    return jnp.concatenate([value, jnp.ones_like(value)], axis=1)


def page_bias(table_ref, length_ref, page, offset):
    positions = table_ref.shape[1]
    length = length_ref[...]
    last = (length - 1) // PAGE
    times = jnp.zeros((length.shape[0], page.shape[1]), jnp.float32)
    tail_page = jnp.zeros_like(length)
    for p in range(positions):
        named = table_ref[:, p : p + 1]
        times = times + jnp.where(page == jnp.where(last > p, named, -1), 1.0, 0.0)
        tail_page = tail_page + jnp.where(last == p, named, 0)
    in_tail = (page == tail_page) & (offset < length - last * PAGE)
    times = times + jnp.where(in_tail, 1.0, 0.0)
    return jnp.where(times > 0.0, jnp.log2(jnp.maximum(times, 1.0)), MASKED)


def pool_kernel(
    query_ref, pool_ref, table_ref, length_ref, adapter_ref, middle_ref, up_ref, base_ref,
    attended_ref, level_ref, bias_ref, pool_bias_ref, split_ref, base_split_ref,
):
    rows = query_ref.shape[0]
    heads = query_ref.shape[1] // HEAD_SIZE
    pool_tokens = pool_ref.shape[0] // 2
    span = 2 * ADAPTER_RANK
    middle = middle_ref[...]
    middle = jnp.concatenate([middle, middle], axis=1)
    lane = lax.broadcasted_iota(jnp.int32, middle.shape, 1)
    mine = (lane // span) == adapter_ref[...]
    half = (lane % span) // ADAPTER_RANK
    base_split_ref[...] = base_ref[...].astype(jnp.float32)
    fresh = []
    for j in range(2):
        picked = jnp.where(mine & (half == j), middle, 0.0).astype(jnp.bfloat16)
        delta = jnp.dot(picked, up_ref[...], preferred_element_type=jnp.float32)
        base = base_split_ref[pl.ds(j, rows, stride=2), :]
        fresh.append((base + ADAPTER_SCALE * delta).astype(jnp.bfloat16).astype(jnp.float32))
    token = lax.broadcasted_iota(jnp.int32, (1, bias_ref.shape[1]), 1)
    page = (pool_tokens + token) // PAGE
    bias_ref[...] = page_bias(table_ref, length_ref, page, token % PAGE)
    token = lax.broadcasted_iota(jnp.int32, (1, pool_tokens), 1)
    pool_bias_ref[...] = page_bias(table_ref, length_ref, token // PAGE, token % PAGE)
    split_ref[...] = pool_ref[...].astype(jnp.float32)
    key = split_ref[pl.ds(0, pool_tokens, stride=2), :].astype(jnp.bfloat16)
    value = with_ones(split_ref[pl.ds(1, pool_tokens, stride=2), :].astype(jnp.bfloat16))
    own_total = with_ones(fresh[1])
    blocks = 2
    tokens = pool_tokens // blocks
    for first in range(0, heads, HEAD_BLOCK):
        query = heads_of(query_ref, first, HEAD_BLOCK)
        own = query.astype(jnp.float32) * jnp.concatenate([fresh[0]] * HEAD_BLOCK, axis=0)
        top = jnp.sum(own, axis=-1, keepdims=True) * SCORE_SCALE
        total = jnp.concatenate([own_total] * HEAD_BLOCK, axis=0)
        for c in range(blocks):
            block = slice(c * tokens, (c + 1) * tokens)
            top, total = attend(query, key[block], value[block], pool_bias_ref[:, block], top, total)
        attended_ref[first * rows : (first + HEAD_BLOCK) * rows] = total[:, :HEAD_SIZE] / total[:, HEAD_SIZE:]
        level = top + jnp.log2(total[:, HEAD_SIZE : HEAD_SIZE + 1])
        for h in range(HEAD_BLOCK):
            level_ref[:, first + h : first + h + 1] = level[h * rows : (h + 1) * rows]


def pool_decode(query, pool, table, length, adapter, middle, up, base, landing_tokens):
    rows, width = query.shape
    stacked = rows * width // HEAD_SIZE
    pool_tokens = pool.shape[0] // 2
    return pl.pallas_call(
        pool_kernel,
        out_shape=(
            jax.ShapeDtypeStruct((stacked, HEAD_SIZE), jnp.float32),
            jax.ShapeDtypeStruct((rows, stacked // rows), jnp.float32),
            jax.ShapeDtypeStruct((rows, landing_tokens), jnp.float32),
        ),
        in_specs=[in_vmem()] * 8,
        out_specs=[in_vmem()] * 3,
        scratch_shapes=[
            pltpu.VMEM((rows, pool_tokens), jnp.float32),
            pltpu.VMEM(pool.shape, jnp.float32),
            pltpu.VMEM(base.shape, jnp.float32),
        ],
        compiler_params=params(),
        cost_estimate=cost(
            stacked * pool_tokens * HEAD_SIZE * 6, pool.size * 2 + stacked * 1536, stacked * pool_tokens
        ),
        name="pool_decode",
    )(query, pool, table, length, adapter, middle, up, base)


def landing_kernel(query_ref, landing_ref, bias_ref, attended_ref, level_ref, out_hbm, out_ref, out_sem):
    rows = query_ref.shape[0]
    heads = query_ref.shape[1] // HEAD_SIZE
    groups, cap, slot_rows, _ = landing_ref.shape
    half = slot_rows // 2
    span = min(groups, LANDING_TOKENS // (cap * half))
    tokens = span * cap * half

    def begin(first):
        query = heads_of(query_ref, first, HEAD_BLOCK)
        top = jnp.concatenate(
            [level_ref[:, h : h + 1] for h in range(first, first + HEAD_BLOCK)], axis=0
        )
        return query, top, with_ones(attended_ref[first * rows : (first + HEAD_BLOCK) * rows])

    def part(c):
        block = slice(c * span, (c + 1) * span)
        key = landing_ref[block, :, :half].reshape(tokens, HEAD_SIZE)
        value = with_ones(landing_ref[block, :, half:].reshape(tokens, HEAD_SIZE))
        return key, value, bias_ref[:, c * tokens : (c + 1) * tokens]

    def finish(first, total):
        result = (total[:, :HEAD_SIZE] / total[:, HEAD_SIZE:]).astype(jnp.bfloat16)
        for h in range(HEAD_BLOCK):
            lanes = slice((first + h) * HEAD_SIZE, (first + h + 1) * HEAD_SIZE)
            out_ref[:, lanes] = result[h * rows : (h + 1) * rows]

    def leave(first):
        lanes = pl.ds(first * HEAD_SIZE, HEAD_BLOCK * HEAD_SIZE)
        return pltpu.make_async_copy(
            out_ref.at[:, lanes], out_hbm.at[:, lanes], out_sem.at[first // HEAD_BLOCK]
        )

    worst = jnp.zeros((8, HEAD_SIZE), jnp.float32)
    for first in range(0, heads, HEAD_BLOCK):
        query, top, total = begin(first)
        top = top.reshape(HEAD_BLOCK, rows, 1)
        for c in range(groups // span):
            key, value, bias = part(c)
            scores = lax.dot_general(query, key, CONTRACT_LAST, preferred_element_type=jnp.float32)
            scores = scores.reshape(HEAD_BLOCK, rows, tokens) * SCORE_SCALE + (bias[None] - top)
            weights = jnp.exp2(scores).astype(jnp.bfloat16).reshape(HEAD_BLOCK * rows, tokens)
            total = total + jnp.dot(weights, value, preferred_element_type=jnp.float32)
        finish(first, total)
        leave(first).start()
        worst = jnp.maximum(worst, jnp.max(total[:, HEAD_SIZE:].reshape(-1, 8, HEAD_SIZE), axis=0))

    for first in range(0, heads, HEAD_BLOCK):
        leave(first).wait()

    @pl.when(jnp.logical_not(jnp.max(worst) < SAFE_TOTAL))
    def _():
        for first in range(0, heads, HEAD_BLOCK):
            query, top, total = begin(first)
            for c in range(groups // span):
                top, total = attend(query, *part(c), top, total)
            finish(first, total)
            leave(first).start()
            leave(first).wait()


def landing_decode(query, landing, bias, attended, level):
    stacked = attended.shape[0]
    tokens = bias.shape[1]
    return pl.pallas_call(
        landing_kernel,
        out_shape=jax.ShapeDtypeStruct(query.shape, jnp.bfloat16),
        in_specs=[in_vmem()] * 5,
        out_specs=pl.BlockSpec(memory_space=pl.ANY),
        scratch_shapes=[
            pltpu.VMEM(query.shape, query.dtype),
            pltpu.SemaphoreType.DMA((query.shape[1] // (HEAD_BLOCK * HEAD_SIZE),)),
        ],
        compiler_params=params(),
        cost_estimate=cost(
            stacked * tokens * HEAD_SIZE * 6, landing.size * 2 + stacked * 1024, stacked * tokens
        ),
        name="landing_decode",
    )(query, landing, bias, attended, level)


def body(
    stretch_query_rows,
    earlier_token_cache,
    stretch_cache,
    stretch_position,
    owning_decode_group,
    decode_query_rows,
    decode_input_rows,
    decode_base_projection,
    row_adapter_index,
    adapter_down_weight,
    adapter_up_weight,
    group_page_store,
    row_page_index,
    cached_token_length,
):
    groups = lax.axis_size("group")
    prompts, stretch_len = stretch_cache.shape[:2]
    prefix_len = earlier_token_cache.shape[1]
    stretch = stretch_cache.reshape(prompts, 2 * stretch_len, HEAD_SIZE)
    earlier = earlier_token_cache.reshape(prompts, 2 * prefix_len, HEAD_SIZE)
    pool = group_page_store.reshape(-1, HEAD_SIZE)
    base = decode_base_projection.reshape(-1, HEAD_SIZE)
    adapter = row_adapter_index[:, None]
    length = cached_token_length[:, None]

    outgoing = pack(owning_decode_group, stretch, groups)
    landing = lax.all_to_all(
        outgoing.reshape(groups, -1, HEAD_SIZE), "group", 0, 0, tiled=True
    ).reshape(outgoing.shape)
    middle = sum_over_tensor(down(decode_input_rows, adapter_down_weight, adapter))
    prefill_out = prefill(stretch_position, stretch_query_rows, earlier, stretch)
    attended, level, bias = pool_decode(
        decode_query_rows, pool, row_page_index, length, adapter, middle, adapter_up_weight, base,
        groups * CAP * stretch_len,
    )
    decode_out = landing_decode(decode_query_rows, landing, bias, attended, level)
    return (prefill_out, decode_out)


def solution(mesh):
    placed = (
        P("group", "tensor"),
        P("group", None, None, "tensor"),
        P("group", None, None, "tensor"),
        P("group"),
        P("group"),
        P("group", "tensor"),
        P("group", "tensor"),
        P("group", None, "tensor"),
        P("group"),
        P("tensor", None),
        P(None, "tensor"),
        P("group", None, None, "tensor"),
        P("group", None),
        P("group"),
    )
    return jax.shard_map(
        body,
        mesh=mesh,
        in_specs=placed,
        out_specs=(P("group", "tensor"), P("group", "tensor")),
        check_vma=False,
    )
```
